256 devices in a mesh: mem: 32 (over z, y), dp: 4 (over x), section: 2 (over core).
Axes of the slice: x: 4, y: 4, z: 8, core: 2. Of those that a mesh axis runs over, the one named last changes fastest.
Arguments:
- layer_input: bfloat16 [2, 16384, 2048], P('section', ('mem', 'dp')), may hold values from -24 to 24
- out_grad: bfloat16 [2, 16384, 2048], P('section', ('mem', 'dp')), may hold values from -6 to 6
- query_weight: bfloat16 [2, 2048, 512], P('section'), may hold values from -0.125 to 0.125
- key_one: float32 [2, 256, 256], P('section'), may hold values from -2 to 2
- key_two: float32 [2, 64, 256], P('section'), may hold values from -2 to 2
- values: bfloat16 [2, 16384, 2048], P('section', 'mem'), may hold values from -0.125 to 0.125
- block_ids: int32 [2, 128, 32], P('section'), may hold values from 0 to 255, as said below
Outputs:
- value_grad: bfloat16 [2, 16384, 2048], P('section', ('mem', 'dp'))
- query_grad: float32 [2, 2048, 512], P('section', ('mem', 'dp'))
- handed_grad: bfloat16 [2, 16384, 2048], P('section', ('mem', 'dp'))
The draws below stay inside these ranges and needn't reach their ends.
Inputs may be any that keep to these rules, and one draw needn't show every extreme that they name: `block_ids`: each row names 32 different blocks; at most 2 of a row's blocks lie in one value shard (blocks m * 8 to m * 8 + 7), and in every row some shard holds exactly 2 of them.
All inputs are finite; a program needn't handle non-finite values.
Results may differ from the reference program's by a relative error of at most 0.006.
Values may be sent and summed in bfloat16 or wider, within the bound.
No kernel may reach another device: no remote copies, remote signals or barrier semaphores. Data moves between devices by JAX's collectives and lax.ppermute only.
A program may use at most 128 MiB of HBM per device.

```python
import math
import jax
import jax.numpy as jnp
from jax import lax

D = 2048
QH = 256
BR = 64
K = 32
BLK_DEV = 8
LAYERS = 2
GROUPS = 128
TOKENS = 16384
NBLK = 256
N_MEM = 32


def draw_block_ids(key, part):
    key = jax.random.fold_in(key, 7)
    capacity = max(2, (K + N_MEM - 1) // N_MEM)
    full_count = K // capacity
    least = max(1, -((N_MEM - K) // (capacity - 1)))

    def one_group(group_key):
        perm_key, heavy_key, shift_key, order_key = jax.random.split(group_key, 4)
        owners = jax.random.permutation(perm_key, N_MEM)
        heavy = jax.random.randint(heavy_key, (), least, full_count + 1)
        shifts = jax.random.randint(shift_key, (N_MEM,), 0, BLK_DEV)
        slots = jnp.arange(K)
        position = jnp.where(slots < heavy * capacity, slots // capacity, heavy + slots - heavy * capacity)
        within = jnp.where(slots < heavy * capacity, slots % capacity, 0)
        owner = owners[position]
        inside = (shifts[owner] + within) % BLK_DEV
        chosen = owner * BLK_DEV + inside
        return chosen[jax.random.permutation(order_key, K)]
    group_keys = jax.random.split(key, LAYERS * GROUPS)
    return jax.vmap(one_group)(group_keys).reshape(LAYERS, GROUPS, K).astype(jnp.int32)


def raised(values, own_key, source, target, blocks, factor):
    owner, partner = [(jnp.arange(values.shape[dim]) // (values.shape[dim] // blocks)).reshape([-1 if axis == dim else 1 for axis in range(values.ndim)]) for dim in (source, target)]
    chosen = jax.random.permutation(own_key, blocks)[partner]
    strong = (owner == chosen) | (owner == (partner + blocks // 2) % blocks)
    return jnp.where(strong, factor * values, values)


def block_scale(key, shape, cuts, low, top_value):
    factor_of, own = 1.0, jax.random.fold_in(key, 6)
    for dim, shards_of in cuts:
        heights = jnp.exp(jax.random.uniform(jax.random.fold_in(own, dim), (shards_of,), jnp.float32, low / len(cuts), top_value / len(cuts)))
        factor_of = factor_of * jnp.repeat(heights, shape[dim] // shards_of).reshape([-1 if axis == dim else 1 for axis in range(len(shape))])
    return factor_of


def gaussian(key, dims, scale, bound, shards=(), kind=jnp.bfloat16):
    entries = scale * jax.random.normal(key, dims, jnp.float32)
    if shards:
        entries = entries * block_scale(key, dims, shards, -0.22, 0.18)
    return jnp.clip(entries, -bound, bound).astype(kind)


def bell_draw_with(key, extent, deviation, reach, cuts, heavy, kind=jnp.bfloat16):
    drawn = deviation * jax.random.normal(key, extent, jnp.float32)
    if cuts:
        drawn = drawn * block_scale(key, extent, cuts, -0.22, 0.18)
    return jnp.clip(raised(drawn, jax.random.fold_in(key, 3), *heavy), -reach, reach).astype(kind)


def setup_inputs(seed: int = 0) -> dict:
    splits = jax.random.split(jax.random.key(seed), 8)
    layer_input = bell_draw_with(splits[0], (LAYERS, TOKENS, D), 1.0, 24.0, ((0, 2), (1, 128)), (1, 2, 128, 5.5))
    out_grad = gaussian(splits[1], (LAYERS, TOKENS, D), 1.0, 6.0, ((0, 2), (1, 128)))
    query_weight = gaussian(splits[2], (LAYERS, D, 2 * QH), D ** -0.5, 0.125, ((0, 2),))
    key_one = jnp.clip(jax.random.uniform(splits[3], (LAYERS, NBLK, QH), jnp.float32, -2.0, 2.0) * block_scale(splits[3], (LAYERS, NBLK, QH), ((0, 2),), -0.4, 0.0), -2.0, 2.0)
    key_two = jnp.clip(jax.random.uniform(splits[4], (LAYERS, BR, QH), jnp.float32, -2.0, 2.0) * block_scale(splits[4], (LAYERS, BR, QH), ((0, 2),), -0.4, 0.0), -2.0, 2.0)
    values = gaussian(splits[5], (LAYERS, NBLK * BR, D), D ** -0.5, 0.125, ((0, 2), (1, 32)))
    block_ids = draw_block_ids(jax.random.fold_in(splits[7], 71), 0)
    return {"layer_input": layer_input, "out_grad": out_grad, "query_weight": query_weight, "key_one": key_one, "key_two": key_two, "values": values, "block_ids": block_ids}


epsilon = 1e-06
highest = lax.Precision.HIGHEST

def query_probs(queries, first_keys, second_keys, half_width):
    factor = 1.0 / math.sqrt(half_width)
    leading = queries[..., :half_width]
    trailing = queries[..., half_width:]
    leading = leading * lax.rsqrt(lax.optimization_barrier(jnp.mean(leading * leading, axis=-1, keepdims=True)) + epsilon)
    trailing = trailing * lax.rsqrt(lax.optimization_barrier(jnp.mean(trailing * trailing, axis=-1, keepdims=True)) + epsilon)
    block_logit = jnp.einsum('ntq,nkq->ntk', leading, first_keys, precision=highest) * factor
    row_logit = jnp.einsum('ntq,rq->ntr', trailing, second_keys, precision=highest) * factor
    block_exp = jnp.exp(block_logit)
    row_exp = jnp.exp(row_logit)
    return (block_exp / lax.optimization_barrier(jnp.sum(block_exp, axis=-1, keepdims=True)), row_exp / lax.optimization_barrier(jnp.sum(row_exp, axis=-1, keepdims=True)))

def layer_backward(inputs, upstream, weight, first_table, second_table, value_table, chosen_ids):
    group_count = chosen_ids.shape[0]
    group_rows = inputs.shape[0] // group_count
    half_width = weight.shape[1] // 2
    block_rows = second_table.shape[0]
    projected = jnp.dot(inputs, weight, preferred_element_type=jnp.float32).astype(jnp.bfloat16)
    widened = lax.optimization_barrier(projected).astype(jnp.float32)
    widened = widened.reshape(group_count, group_rows, 2 * half_width)
    group_keys = first_table[chosen_ids]

    def both_probs(queries):
        return query_probs(queries, group_keys, second_table, half_width)
    (block_probs, row_probs), pullback = jax.vjp(both_probs, widened)
    grouped = upstream.reshape(group_count, group_rows, -1)
    offsets = jnp.arange(block_rows, dtype=jnp.int32)

    def one_group(totals, members):
        up_rows, block_part, row_part, group_ids = members
        table_rows = (group_ids[:, None] * block_rows + offsets[None, :]).reshape(-1).astype(jnp.int32)
        picked = value_table[table_rows]
        products = jnp.dot(up_rows, picked.T, preferred_element_type=jnp.float32)
        weight_tiles = (block_part[:, :, None] * row_part[:, None, :]).astype(jnp.bfloat16)
        weight_tiles = weight_tiles.reshape(group_rows, -1)
        totals = totals.at[table_rows].add(jnp.dot(weight_tiles.T, up_rows, preferred_element_type=jnp.float32))
        return (totals, products)
    start_totals = jnp.zeros(value_table.shape, jnp.float32)
    totals, products = lax.scan(one_group, start_totals, (grouped, block_probs, row_probs, chosen_ids))
    products = products.reshape(group_count, group_rows, -1, block_rows)
    block_cot = jnp.einsum('gtkr,gtr->gtk', products, row_probs, precision=highest)
    row_cot = jnp.einsum('gtkr,gtk->gtr', products, block_probs, precision=highest)
    grad_query = pullback((block_cot, row_cot))[0].reshape(inputs.shape[0], -1).astype(jnp.bfloat16)
    weight_grad = jnp.dot(inputs.T, grad_query, preferred_element_type=jnp.float32)
    input_grad = jnp.dot(grad_query, weight.T, preferred_element_type=jnp.float32).astype(jnp.bfloat16)
    return (totals.astype(jnp.bfloat16), weight_grad, input_grad)

def reference(layer_input, out_grad, query_weight, key_one, key_two, values, block_ids):
    outcomes = [layer_backward(layer_input[layer], out_grad[layer], query_weight[layer], key_one[layer], key_two[layer], values[layer], block_ids[layer]) for layer in range(LAYERS)]
    value_grad = jnp.stack([outcome[0] for outcome in outcomes])
    query_grad = jnp.stack([outcome[1] for outcome in outcomes])
    handed_grad = jnp.stack([outcomes[layer ^ 1][2] for layer in range(LAYERS)])
    return (value_grad, query_grad, handed_grad)
```

```python
import functools
import math

import jax
import jax.numpy as jnp
from jax import lax
from jax.experimental import pallas as pl
from jax.experimental.pallas import tpu as pltpu
from jax.sharding import PartitionSpec as P

EPS = 1e-06
HIGHEST = lax.Precision.HIGHEST
VMEM = pl.BlockSpec(memory_space=pltpu.VMEM)
SMEM = pl.BlockSpec(memory_space=pltpu.SMEM)
NT = (((1,), (1,)), ((), ()))
Y = 4


def shift_mem(block, dz, dy):
    count = lax.axis_size("mem")
    depth = count // Y
    route = []
    for z in range(depth):
        for y in range(Y):
            route.append((z * Y + y, ((z + dz) % depth) * Y + (y + dy) % Y))
    return lax.ppermute(block, "mem", route)


def shift_dp(block, step):
    count = lax.axis_size("dp")
    return lax.ppermute(block, "dp", [(i, (i + step) % count) for i in range(count)])


def normed(part):
    scale = lax.rsqrt(jnp.mean(part * part, axis=0, keepdims=True) + EPS)
    return part * scale, scale


def head_kernel(ids, x_ref, w_ref, k1_ref, k2_ref, probs_ref, q_ref, keys_ref):
    picks, half = keys_ref.shape
    q = jnp.dot(x_ref[...], w_ref[...], preferred_element_type=jnp.float32)
    q = q.astype(jnp.bfloat16).astype(jnp.float32)
    q_t = q.T
    q_ref[...] = q_t
    for k in range(picks):
        keys_ref[k : k + 1, :] = k1_ref[pl.ds(ids[k], 1), :]
    factor = 1.0 / math.sqrt(half)
    first, _ = normed(q_t[:half])
    second, _ = normed(q_t[half:])
    block_exp = jnp.exp(
        jnp.dot(keys_ref[...], first, precision=HIGHEST, preferred_element_type=jnp.float32) * factor
    )
    row_exp = jnp.exp(
        jnp.dot(k2_ref[...], second, precision=HIGHEST, preferred_element_type=jnp.float32) * factor
    )
    probs_ref[:picks, :] = block_exp / jnp.sum(block_exp, axis=0, keepdims=True)
    probs_ref[picks:, :] = row_exp / jnp.sum(row_exp, axis=0, keepdims=True)


def tail_kernel(ids, recv_ref, probs_ref, q_ref, keys_ref, k2_ref, out_ref, cot_ref):
    picks, half = keys_ref.shape
    rows = k2_ref.shape[0]
    per_owner = recv_ref.shape[1] - rows
    factor = 1.0 / math.sqrt(half)
    row_cot = jnp.sum(recv_ref[:, :rows, :], axis=0)
    for k in range(picks):
        owner = ids[k] // per_owner
        inside = ids[k] % per_owner
        cot_ref[k : k + 1, :] = recv_ref[owner, pl.ds(rows + inside, 1), :]
    block_cot = cot_ref[...]
    q_t = q_ref[...]

    def through(part, probs, cot, keys):
        unit, scale = normed(part)
        logit_cot = probs * (cot - jnp.sum(probs * cot, axis=0, keepdims=True)) * factor
        unit_cot = jnp.dot(
            keys.T, logit_cot, precision=HIGHEST, preferred_element_type=jnp.float32
        )
        inner = jnp.mean(unit * unit_cot, axis=0, keepdims=True)
        return scale * (unit_cot - unit * inner)

    lead = through(q_t[:half], probs_ref[:picks, :], block_cot, keys_ref[...])
    trail = through(q_t[half:], probs_ref[picks:, :], row_cot, k2_ref[...])
    out_ref[:, :half] = lead.T.astype(jnp.bfloat16)
    out_ref[:, half:] = trail.T.astype(jnp.bfloat16)


def chunk_kernel(count, rows, group_rows, *refs):
    numbers = refs[0]
    chunks = refs[1 : 1 + count]
    v_ref, probs_ref, vg_in, ret_in, vg_out, ret_out, tile_ref = refs[1 + count :]
    per_owner = v_ref.shape[0] // rows
    ret_out[...] = ret_in[...]
    place = 0
    for part, chunk in enumerate(chunks):
        groups = chunk.shape[0] // group_rows
        for pair in range(0, groups, 2):
            start = pair * group_rows
            wide = 2 * group_rows
            up = chunk[start : start + wide, :]
            products = lax.dot_general(
                v_ref[...], up, NT, preferred_element_type=jnp.float32
            )
            for j in range(2):
                g = numbers[place]
                place += 1
                row_probs = probs_ref[g, :rows, :]
                slot_probs = probs_ref[g, rows:, :]
                row_part = ret_out[g, :rows, :]
                slot_parts = []
                for b in range(per_owner):
                    piece = products[b * rows : (b + 1) * rows, j * group_rows : (j + 1) * group_rows]
                    one = slot_probs[b : b + 1, :]
                    row_part = row_part + piece * one
                    slot_parts.append(jnp.sum(piece * row_probs, axis=0, keepdims=True))
                    tile_ref[
                        b * rows : (b + 1) * rows,
                        start + j * group_rows : start + (j + 1) * group_rows,
                    ] = (one * row_probs).astype(jnp.bfloat16)
                ret_out[g, :rows, :] = row_part
                ret_out[g, rows:, :] = ret_out[g, rows:, :] + jnp.concatenate(slot_parts, axis=0)
        before = vg_in if part == 0 else vg_out
        vg_out[...] = before[...] + jnp.dot(
            tile_ref[:, : groups * group_rows], chunk[...], preferred_element_type=jnp.float32
        )


def chunk_step(numbers, chunks, half_values, probs, state, rows, group_rows):
    vg, ret = state
    count = len(chunks)
    longest = max(chunk.shape[0] for chunk in chunks)
    tokens = sum(chunk.shape[0] for chunk in chunks)
    flops = 4 * tokens * half_values.shape[0] * half_values.shape[1]
    moved = 2 * (vg.size * 4 + ret.size * 4) + probs.size * 4 + half_values.size * 2
    return pl.pallas_call(
        functools.partial(chunk_kernel, count, rows, group_rows),
        out_shape=(
            jax.ShapeDtypeStruct(vg.shape, vg.dtype),
            jax.ShapeDtypeStruct(ret.shape, ret.dtype),
        ),
        in_specs=[SMEM] + [VMEM] * (count + 4),
        out_specs=(VMEM, VMEM),
        scratch_shapes=[pltpu.VMEM((half_values.shape[0], longest), jnp.bfloat16)],
        input_output_aliases={count + 3: 0, count + 4: 1},
        compiler_params=pltpu.CompilerParams(vmem_limit_bytes=40 * 1024 * 1024),
        cost_estimate=pl.CostEstimate(flops=flops, bytes_accessed=moved, transcendentals=0),
        name="chunk",
    )(numbers, *chunks, half_values, probs, vg, ret)


def shards(layer_input, out_grad, query_weight, key_one, key_two, values, block_ids):
    tokens = layer_input[0]
    upstream = out_grad[0]
    weight = query_weight[0]
    first_table = key_one[0]
    second_table = key_two[0]
    all_ids = block_ids[0]
    group_rows, width = tokens.shape
    half = weight.shape[1] // 2
    rows = second_table.shape[0]
    per_owner = values.shape[1] // rows
    picks = all_ids.shape[1]
    mem_count = lax.axis_size("mem")
    dp_count = lax.axis_size("dp")
    depth = mem_count // Y
    mem_index = lax.axis_index("mem")
    dp_index = lax.axis_index("dp")
    z_index = mem_index // Y
    y_index = mem_index % Y
    own_ids = lax.dynamic_index_in_dim(all_ids, mem_index * dp_count + dp_index, 0, keepdims=False)
    cols = width // 2
    left = upstream[:, :cols]
    right = upstream[:, cols:]
    mid = group_rows // 2

    probs, q_t, own_keys = pl.pallas_call(
        head_kernel,
        out_shape=(
            jax.ShapeDtypeStruct((picks + rows, group_rows), jnp.float32),
            jax.ShapeDtypeStruct((2 * half, group_rows), jnp.float32),
            jax.ShapeDtypeStruct((picks, half), jnp.float32),
        ),
        in_specs=[SMEM, VMEM, VMEM, VMEM, VMEM],
        out_specs=(VMEM, VMEM, VMEM),
        compiler_params=pltpu.CompilerParams(vmem_limit_bytes=24 * 1024 * 1024),
        name="head",
    )(own_ids, tokens, weight, first_table, second_table)
    all_probs = lax.all_gather(probs, "mem", axis=0)
    plane_ids = all_ids.reshape(mem_count, dp_count, picks)
    plane_ids = lax.dynamic_index_in_dim(plane_ids, dp_index, 1, keepdims=False)
    local = mem_index * per_owner + jnp.arange(per_owner)
    chosen = (plane_ids[:, None, :] == local[None, :, None]).astype(jnp.float32)
    slot_probs = jnp.einsum("gbk,gkt->gbt", chosen, all_probs[:, :picks], precision=HIGHEST)
    tables = jnp.concatenate([all_probs[:, picks:], slot_probs], axis=1)

    def number(dz, dy):
        return ((z_index + dz + depth) % depth) * Y + (y_index + dy + Y) % Y

    z_order = [0, -1, 1, -2, 2, -3, 3, 4]
    y_order = [0, -1, 1, 2]

    yp = shift_mem(left, 0, 1)
    ym = shift_mem(left, 0, -1)
    zp = shift_mem(right, 1, 0)
    zm = shift_mem(right, -1, 0)
    y2p = shift_mem(yp[:mid], 0, 1)
    y2m = shift_mem(ym[mid:], 0, -1)
    y_block = jnp.concatenate([left, yp, ym, y2p, y2m], axis=0)
    pieces = [right, zp, zm]
    for _ in range(2):
        zp = shift_mem(zp, 1, 0)
        zm = shift_mem(zm, -1, 0)
        pieces += [zp, zm]
    pieces.append(shift_mem(zp[:mid], 1, 0))
    pieces.append(shift_mem(zm[mid:], -1, 0))
    z_block = jnp.concatenate(pieces, axis=0)

    step = functools.partial(chunk_step, rows=rows, group_rows=group_rows)
    left_values = values[0][:, :cols]
    right_values = values[0][:, cols:]
    zero_ret = jnp.zeros((mem_count, rows + per_owner, group_rows), jnp.float32)
    left_state = (jnp.zeros((per_owner * rows, cols), jnp.float32), zero_ret)
    right_state = (jnp.zeros((per_owner * rows, cols), jnp.float32), zero_ret)

    def numbers(pairs):
        return jnp.stack([number(dz, dy) for dz, dy in pairs]).astype(jnp.int32)

    wp = shift_mem(y_block, 1, 0)
    wm = shift_mem(y_block, -1, 0)
    gp = shift_mem(z_block, 0, 1)
    gm = shift_mem(z_block, 0, -1)
    left_state = step(numbers([(0, dy) for dy in y_order]), [y_block], left_values, tables, left_state)
    right_state = step(numbers([(dz, 0) for dz in z_order]), [z_block], right_values, tables, right_state)
    for far in range(1, depth // 2):
        pairs = [(-far, dy) for dy in y_order] + [(far, dy) for dy in y_order]
        if far == depth // 2 - 1:
            np_ = shift_mem(wp[: 2 * group_rows], 1, 0)
            nm_ = shift_mem(wm[2 * group_rows :], -1, 0)
        else:
            np_ = shift_mem(wp, 1, 0)
            nm_ = shift_mem(wm, -1, 0)
        left_state = step(numbers(pairs), [wp, wm], left_values, tables, left_state)
        wp, wm = np_, nm_
    hp = shift_mem(gp[: 4 * group_rows], 0, 1)
    hm = shift_mem(gm[4 * group_rows :], 0, -1)
    right_state = step(numbers([(dz, -1) for dz in z_order]), [gp], right_values, tables, right_state)
    right_state = step(numbers([(dz, 1) for dz in z_order]), [gm], right_values, tables, right_state)
    left_state = step(
        numbers([(4, dy) for dy in y_order]), [wp, wm], left_values, tables, left_state
    )
    right_state = step(
        numbers([(dz, 2) for dz in z_order]), [hp, hm], right_values, tables, right_state
    )

    received = lax.all_to_all(left_state[1] + right_state[1], "mem", 0, 0, tiled=True)
    query_cot = pl.pallas_call(
        tail_kernel,
        out_shape=jax.ShapeDtypeStruct((group_rows, 2 * half), jnp.bfloat16),
        in_specs=[SMEM] + [VMEM] * 5,
        out_specs=VMEM,
        scratch_shapes=[pltpu.VMEM((picks, group_rows), jnp.float32)],
        compiler_params=pltpu.CompilerParams(vmem_limit_bytes=24 * 1024 * 1024),
        name="tail",
    )(own_ids, received, probs, q_t, own_keys, second_table)

    turned = tokens.T.reshape(mem_count, dp_count, width // (mem_count * dp_count), group_rows)
    turned = turned.transpose(1, 0, 2, 3).reshape(dp_count, width // dp_count, group_rows)

    def piece(offset):
        return lax.dynamic_index_in_dim(turned, (dp_index + offset) % dp_count, 0, keepdims=False)

    inputs = [piece(0)] + [shift_dp(piece(d), d) for d in (1, 2, 3)]
    cots = [query_cot] + [shift_dp(query_cot, d) for d in (1, 2, 3)]
    partial_grad = jnp.dot(
        jnp.concatenate(inputs, axis=1),
        jnp.concatenate(cots, axis=0),
        preferred_element_type=jnp.float32,
    )
    spread = lax.all_to_all(
        partial_grad.reshape(mem_count, -1, 2 * half), "mem", 0, 0, tiled=True
    )
    query_grad = jnp.sum(spread, axis=0)

    def half_sum(total):
        total = total.reshape(dp_count, -1, total.shape[-1])

        def part(offset):
            return lax.dynamic_index_in_dim(
                total, (dp_index + offset + dp_count) % dp_count, 0, keepdims=False
            )

        far = part(2)
        cut = far.shape[1] // 2
        fp = shift_dp(far[:, :cut].astype(jnp.bfloat16), 1).astype(jnp.float32)
        fm = shift_dp(far[:, cut:].astype(jnp.bfloat16), -1).astype(jnp.float32)
        up = part(1)
        down = part(-1)
        up = jnp.concatenate([up[:, :cut] + fp, up[:, cut:]], axis=1).astype(jnp.bfloat16)
        down = jnp.concatenate([down[:, :cut], down[:, cut:] + fm], axis=1).astype(jnp.bfloat16)
        gp_ = shift_dp(up, 1).astype(jnp.float32)
        gm_ = shift_dp(down, -1).astype(jnp.float32)
        return (part(0) + gp_ + gm_).astype(jnp.bfloat16)

    value_grad = jnp.concatenate([half_sum(left_state[0]), half_sum(right_state[0])], axis=1)

    input_grad = lax.dot_general(query_cot, weight, NT, preferred_element_type=jnp.float32)
    handed = lax.ppermute(input_grad.astype(jnp.bfloat16), "section", [(0, 1), (1, 0)])
    return (value_grad[None], query_grad[None], handed[None])


def solution(mesh):
    placed = (
        P("section", ("mem", "dp"), None),
        P("section", ("mem", "dp"), None),
        P("section", None, None),
        P("section", None, None),
        P("section", None, None),
        P("section", "mem", None),
        P("section", None, None),
    )
    return jax.shard_map(
        shards,
        mesh=mesh,
        in_specs=placed,
        out_specs=(
            P("section", ("mem", "dp"), None),
            P("section", ("mem", "dp"), None),
            P("section", ("mem", "dp"), None),
        ),
        check_vma=False,
    )
```

```python
import functools
import math

import jax
import jax.numpy as jnp
from jax import lax
from jax.experimental import pallas as pl
from jax.experimental.pallas import tpu as pltpu
from jax.sharding import PartitionSpec as P

EPS = 1e-06
HIGHEST = lax.Precision.HIGHEST
VMEM = pl.BlockSpec(memory_space=pltpu.VMEM)
SMEM = pl.BlockSpec(memory_space=pltpu.SMEM)
NT = (((1,), (1,)), ((), ()))
Y = 4
TAIL = 16
LANES = 128


def shift_mem(block, dz, dy):
    count = lax.axis_size("mem")
    depth = count // Y
    route = []
    for z in range(depth):
        for y in range(Y):
            route.append((z * Y + y, ((z + dz) % depth) * Y + (y + dy) % Y))
    return lax.ppermute(block, "mem", route)


def shift_dp(block, step):
    count = lax.axis_size("dp")
    return lax.ppermute(block, "dp", [(i, (i + step) % count) for i in range(count)])


def normed(part):
    scale = lax.rsqrt(jnp.mean(part * part, axis=0, keepdims=True) + EPS)
    return part * scale, scale


def head_kernel(ids, x_ref, w_ref, k1_ref, k2_ref, up_ref, probs_ref, q_ref, keys_ref, load_ref):
    picks, half = keys_ref.shape
    q = jnp.dot(x_ref[...], w_ref[...], preferred_element_type=jnp.float32)
    q = q.astype(jnp.bfloat16).astype(jnp.float32)
    q_t = q.T
    q_ref[...] = q_t
    for k in range(picks):
        keys_ref[k : k + 1, :] = k1_ref[pl.ds(ids[k], 1), :]
    factor = 1.0 / math.sqrt(half)
    first, _ = normed(q_t[:half])
    second, _ = normed(q_t[half:])
    block_exp = jnp.exp(
        jnp.dot(keys_ref[...], first, precision=HIGHEST, preferred_element_type=jnp.float32) * factor
    )
    row_exp = jnp.exp(
        jnp.dot(k2_ref[...], second, precision=HIGHEST, preferred_element_type=jnp.float32) * factor
    )
    probs_ref[:picks, :] = block_exp / jnp.sum(block_exp, axis=0, keepdims=True)
    probs_ref[picks:, :] = row_exp / jnp.sum(row_exp, axis=0, keepdims=True)
    tokens = up_ref.shape[0]
    load_ref[:tokens, :] = up_ref[...]
    load_ref[tokens:, :] = jnp.zeros((TAIL, up_ref.shape[1]), jnp.bfloat16)
    tiles = probs_ref.shape[0] // TAIL
    for i in range(tiles):
        tile = probs_ref[i * TAIL : (i + 1) * TAIL, :]
        high = tile.astype(jnp.bfloat16)
        low = (tile - high.astype(jnp.float32)).astype(jnp.bfloat16)
        load_ref[tokens:, i * LANES : (i + 1) * LANES] = high
        load_ref[tokens:, (tiles + i) * LANES : (tiles + i + 1) * LANES] = low


def tail_kernel(source, place, recv_ref, probs_ref, q_ref, keys_ref, k2_ref, out_ref, cot_ref):
    picks, half = keys_ref.shape
    rows = k2_ref.shape[0]
    factor = 1.0 / math.sqrt(half)
    row_cot = jnp.sum(recv_ref[:, :rows, :], axis=0)
    for k in range(picks):
        cot_ref[k : k + 1, :] = recv_ref[source[k], pl.ds(rows + place[k], 1), :]
    block_cot = cot_ref[...]
    q_t = q_ref[...]

    def through(part, probs, cot, keys):
        unit, scale = normed(part)
        logit_cot = probs * (cot - jnp.sum(probs * cot, axis=0, keepdims=True)) * factor
        unit_cot = jnp.dot(
            keys.T, logit_cot, precision=HIGHEST, preferred_element_type=jnp.float32
        )
        inner = jnp.mean(unit * unit_cot, axis=0, keepdims=True)
        return scale * (unit_cot - unit * inner)

    lead = through(q_t[:half], probs_ref[:picks, :], block_cot, keys_ref[...])
    trail = through(q_t[half:], probs_ref[picks:, :], row_cot, k2_ref[...])
    out_ref[:, :half] = lead.T.astype(jnp.bfloat16)
    out_ref[:, half:] = trail.T.astype(jnp.bfloat16)


def table_kernel(chosen_ref, low_ref, rp_ref, *slot_refs):
    picks = chosen_ref.shape[2]
    tiles = (picks + rp_ref.shape[1]) // TAIL
    each = slot_refs[0].shape[1]
    for g in range(low_ref.shape[0]):

        def tile(i):
            high = low_ref[g, :, i * LANES : (i + 1) * LANES].astype(jnp.float32)
            rest = low_ref[g, :, (tiles + i) * LANES : (tiles + i + 1) * LANES]
            return high + rest.astype(jnp.float32)

        first = picks // TAIL
        block_probs = jnp.concatenate([tile(i) for i in range(first)], axis=0)
        for i in range(first, tiles):
            rp_ref[g, (i - first) * TAIL : (i - first + 1) * TAIL, :] = tile(i)
        slots = jnp.dot(
            chosen_ref[g], block_probs, precision=HIGHEST, preferred_element_type=jnp.float32
        )
        for n, ref in enumerate(slot_refs):
            ref[g] = slots[n * each : (n + 1) * each]


def return_kernel(count, rows, group_rows, up_ref, rp_ref, sp_ref, *refs):
    pieces = refs[:count]
    out_ref, pair_ref = refs[count:]

    @pl.loop(0, up_ref.shape[0] // 2)
    def _(pair):
        pair_ref[:group_rows, :] = up_ref[pair * 2, :group_rows, :]
        pair_ref[group_rows:, :] = up_ref[pair * 2 + 1, :group_rows, :]
        up = pair_ref[...]
        for j in range(2):
            out_ref[pair * 2 + j, :rows, :] = jnp.zeros((rows, group_rows), jnp.float32)
        slot = 0
        for piece in pieces:
            products = lax.dot_general(piece[...], up, NT, preferred_element_type=jnp.float32)
            blocks = piece.shape[0] // rows
            for j in range(2):
                g = pair * 2 + j
                row_probs = rp_ref[g]
                total = out_ref[g, :rows, :]
                for b in range(blocks):
                    part = products[
                        b * rows : (b + 1) * rows, j * group_rows : (j + 1) * group_rows
                    ]
                    total = total + part * sp_ref[g, slot + b : slot + b + 1, :]
                    out_ref[g, rows + slot + b : rows + slot + b + 1, :] = jnp.sum(
                        part * row_probs, axis=0, keepdims=True
                    )
                out_ref[g, :rows, :] = total
            slot += blocks


def sum_kernel(rows, rp_ref, sp_ref, up_ref, out_ref, tile_ref, flat_ref):
    groups = rp_ref.shape[0]
    group_rows = rp_ref.shape[2]

    @pl.when(pl.program_id(0) == 0)
    def _():
        for g in range(groups):
            flat_ref[g * group_rows : (g + 1) * group_rows, :] = up_ref[g, :group_rows, :]

    for g in range(groups):
        row_probs = rp_ref[g]
        for b in range(sp_ref.shape[1]):
            tile_ref[b * rows : (b + 1) * rows, g * group_rows : (g + 1) * group_rows] = (
                sp_ref[g, b : b + 1, :] * row_probs
            ).astype(jnp.bfloat16)
    out_ref[...] = jnp.dot(
        tile_ref[...], flat_ref[...], preferred_element_type=jnp.float32
    ).astype(jnp.bfloat16)


def value_sums(row_probs, slot_probs, up, part):
    groups, rows, group_rows = row_probs.shape
    blocks = slot_probs.shape[1]
    tokens = groups * group_rows
    cols = up.shape[2] // 2
    each = 8
    return pl.pallas_call(
        functools.partial(sum_kernel, rows),
        out_shape=jax.ShapeDtypeStruct((blocks * rows, cols), jnp.bfloat16),
        grid=(blocks // each,),
        in_specs=[
            pl.BlockSpec((groups, rows, group_rows), lambda i: (0, 0, 0)),
            pl.BlockSpec((groups, each, group_rows), lambda i: (0, i, 0)),
            pl.BlockSpec((groups, up.shape[1], cols), lambda i: (0, 0, part)),
        ],
        out_specs=pl.BlockSpec((each * rows, cols), lambda i: (i, 0)),
        scratch_shapes=[
            pltpu.VMEM((each * rows, tokens), jnp.bfloat16),
            pltpu.VMEM((tokens, cols), jnp.bfloat16),
        ],
        compiler_params=pltpu.CompilerParams(vmem_limit_bytes=32 * 1024 * 1024),
        cost_estimate=pl.CostEstimate(
            flops=2 * blocks * rows * tokens * cols,
            bytes_accessed=2 * (tokens * cols + blocks * rows * cols),
            transcendentals=0,
        ),
        name="value_sums",
    )(row_probs, slot_probs, up)


def ring_gather(block, shift):
    low = shift(block, 1)
    high = shift(block, -1)
    cut = block.shape[0] // 2
    far = (shift(low[:cut], 1), shift(high[cut:], -1))
    return low, high, far


def wide(a):
    return a.astype(jnp.float32)


def ring_far(parts, shift):
    cut = parts.shape[1] // 2
    return shift(parts[2, :cut], 1), shift(parts[2, cut:], -1)


def ring_mix(parts, far):
    cut = parts.shape[1] // 2
    up = jnp.concatenate(
        [(wide(parts[1, :cut]) + wide(far[0])).astype(jnp.bfloat16), parts[1, cut:]], axis=0
    )
    down = jnp.concatenate(
        [parts[3, :cut], (wide(parts[3, cut:]) + wide(far[1])).astype(jnp.bfloat16)], axis=0
    )
    return up, down


def ring_end(parts, mixed, shift):
    return wide(parts[0]) + wide(shift(mixed[0], 1)) + wide(shift(mixed[1], -1))


def ring_sum(parts, shift):
    return ring_end(parts, ring_mix(parts, ring_far(parts, shift)), shift)


def shards(layer_input, out_grad, query_weight, key_one, key_two, values, block_ids):
    tokens = layer_input[0]
    upstream = out_grad[0]
    weight = query_weight[0]
    first_table = key_one[0]
    second_table = key_two[0]
    all_ids = block_ids[0]
    group_rows, width = tokens.shape
    half = weight.shape[1] // 2
    rows = second_table.shape[0]
    per_owner = values.shape[1] // rows
    picks = all_ids.shape[1]
    mem_count = lax.axis_size("mem")
    dp_count = lax.axis_size("dp")
    depth = mem_count // Y
    mem_index = lax.axis_index("mem")
    dp_index = lax.axis_index("dp")
    z_index = mem_index // Y
    y_index = mem_index % Y
    own_ids = lax.dynamic_index_in_dim(all_ids, mem_index * dp_count + dp_index, 0, keepdims=False)
    cols = width // 2
    line = [[z * Y + y for z in range(depth)] for y in range(Y)]
    along_y = lambda block, step: shift_mem(block, 0, step)


    own_values = values[0]
    direct_rows = 4 * rows
    one_block = lax.dynamic_slice_in_dim(own_values, direct_rows + dp_index * rows, rows, 0)
    one_block, tokens = lax.optimization_barrier((one_block, tokens))
    low_b, high_b, far_b = ring_gather(one_block, along_y)
    direct, far_b = lax.optimization_barrier((own_values[:direct_rows], far_b))
    low_d = along_y(direct, 1)
    high_d = along_y(direct, -1)
    spread_x = jnp.concatenate([low_b, high_b, *far_b], axis=0)

    probs, q_t, own_keys, load = pl.pallas_call(
        head_kernel,
        out_shape=(
            jax.ShapeDtypeStruct((picks + rows, group_rows), jnp.float32),
            jax.ShapeDtypeStruct((2 * half, group_rows), jnp.float32),
            jax.ShapeDtypeStruct((picks, half), jnp.float32),
            jax.ShapeDtypeStruct((group_rows + TAIL, width), jnp.bfloat16),
        ),
        in_specs=[SMEM] + [VMEM] * 5,
        out_specs=(VMEM,) * 4,
        compiler_params=pltpu.CompilerParams(vmem_limit_bytes=24 * 1024 * 1024),
        name="head",
    )(own_ids, tokens, weight, first_table, second_table, upstream)

    gathered = lax.all_gather(load, "mem", axis=0, axis_index_groups=line)

    cut = direct_rows // 2
    far_d = (along_y(low_d[:cut], 1), along_y(high_d[cut:], -1))
    low_x = shift_dp(spread_x, 1)
    high_x = shift_dp(spread_x, -1)
    late_tokens, low_x, high_x = lax.optimization_barrier((tokens, low_x, high_x))
    cut = spread_x.shape[0] // 2
    far_x = (shift_dp(low_x[:cut], 1), shift_dp(high_x[cut:], -1))

    y_at = (y_index + jnp.arange(Y)) % Y
    x_at = (dp_index + jnp.arange(dp_count)) % dp_count
    shard_base = (z_index * Y + y_at) * per_owner
    per_x = per_owner // dp_count
    x_blocks = x_at[:, None] * per_x + jnp.arange(per_x)[None, :]
    y_first = (shard_base[:, None, None] + x_blocks[None, :, :]).reshape(-1)
    x_first = (shard_base[None, :, None] + x_blocks[:, None, :]).reshape(-1)
    octets = shard_base[jnp.array([3, 1, 2])]
    x_held = x_at[jnp.array([0, 3, 1, 2])]
    held = jnp.concatenate(
        [
            shard_base[0] + jnp.arange(per_owner),
            (octets[:, None] + jnp.arange(4)[None, :]).reshape(-1),
            (octets[None, :] + 4 + x_held[:, None]).reshape(-1),
        ]
    )
    wanted = jnp.concatenate([held, x_first, y_first])
    cells = all_ids.reshape(depth, Y * dp_count, picks)
    line_ids = lax.dynamic_index_in_dim(cells, y_index * dp_count + dp_index, 1, keepdims=False)
    chosen = (line_ids[:, None, :] == wanted[None, :, None]).astype(jnp.float32)
    count = Y * per_owner
    slots = jax.ShapeDtypeStruct((depth, count, group_rows), jnp.float32)
    row_probs, held_probs, left_probs, right_probs = pl.pallas_call(
        table_kernel,
        out_shape=(jax.ShapeDtypeStruct((depth, rows, group_rows), jnp.float32),) + (slots,) * 3,
        grid=(1,),
        in_specs=[
            pl.BlockSpec(chosen.shape, lambda i: (0, 0, 0)),
            pl.BlockSpec((depth, TAIL, width), lambda i: (0, group_rows // TAIL, 0)),
        ],
        out_specs=(
            pl.BlockSpec((depth, rows, group_rows), lambda i: (0, 0, 0)),
        )
        + (pl.BlockSpec(slots.shape, lambda i: (0, 0, 0)),) * 3,
        name="tables",
    )(chosen, gathered)
    left_sums = value_sums(row_probs, left_probs, gathered, 0)
    right_sums = value_sums(row_probs, right_probs, gathered, 1)

    turned = late_tokens.T.reshape(mem_count, dp_count, width // (mem_count * dp_count), group_rows)
    turned = turned.transpose(1, 0, 2, 3).reshape(dp_count, width // dp_count, group_rows)

    def piece(offset):
        return lax.dynamic_index_in_dim(turned, (dp_index + offset) % dp_count, 0, keepdims=False)

    inputs = [piece(0)] + [shift_dp(piece(d), d) for d in (1, 2, 3)]
    inputs = jnp.concatenate(inputs, axis=1)
    left_parts = left_sums.reshape(dp_count, -1, cols)
    right_parts = right_sums.reshape(Y, -1, cols)
    left_far = ring_far(left_parts, shift_dp)
    right_far = ring_far(right_parts, along_y)
    left_mixed = ring_mix(left_parts, left_far)
    held_probs, inputs, left_mixed = lax.optimization_barrier((held_probs, inputs, left_mixed))
    left_sums, far_d, far_x = lax.optimization_barrier((left_sums, far_d, far_x))
    value_pieces = [own_values, low_d, high_d, *far_d, spread_x, low_x, high_x]
    value_pieces.append(jnp.concatenate(far_x, axis=0))

    returned = pl.pallas_call(
        functools.partial(return_kernel, len(value_pieces), rows, group_rows),
        out_shape=jax.ShapeDtypeStruct((depth, rows + count, group_rows), jnp.float32),
        in_specs=[VMEM] * (3 + len(value_pieces)),
        out_specs=VMEM,
        scratch_shapes=[pltpu.VMEM((2 * group_rows, width), jnp.bfloat16)],
        compiler_params=pltpu.CompilerParams(vmem_limit_bytes=40 * 1024 * 1024),
        cost_estimate=pl.CostEstimate(
            flops=2 * depth * group_rows * count * rows * width,
            bytes_accessed=2 * (depth * group_rows + count * rows) * width,
            transcendentals=0,
        ),
        name="returns",
    )(gathered, row_probs, held_probs, *value_pieces)

    received = lax.all_to_all(returned, "mem", 0, 0, tiled=True, axis_index_groups=line)
    source = own_ids // count
    dy = (own_ids // per_owner - y_index + Y) % Y
    inside = own_ids % per_owner
    octet = jnp.array([0, 1, 2, 0])[dy]
    x_slot = jnp.array([0, 2, 3, 1])[(inside - 4 - dp_index + 2 * dp_count) % dp_count]
    place = jnp.where(
        dy == 0,
        inside,
        jnp.where(inside < 4, per_owner + octet * 4 + inside, per_owner + 12 + x_slot * 3 + octet),
    )
    left_x = ring_end(left_parts, left_mixed, shift_dp).astype(jnp.bfloat16)
    right_mixed = ring_mix(right_parts, right_far)
    right_y = ring_end(right_parts, right_mixed, along_y).astype(jnp.bfloat16)
    received, left_x, right_y = lax.optimization_barrier((received, left_x, right_y))
    query_cot = pl.pallas_call(
        tail_kernel,
        out_shape=jax.ShapeDtypeStruct((group_rows, 2 * half), jnp.bfloat16),
        in_specs=[SMEM, SMEM] + [VMEM] * 5,
        out_specs=VMEM,
        scratch_shapes=[pltpu.VMEM((picks, group_rows), jnp.float32)],
        compiler_params=pltpu.CompilerParams(vmem_limit_bytes=24 * 1024 * 1024),
        name="tail",
    )(source, place, received, probs, q_t, own_keys, second_table)

    cots = [query_cot] + [shift_dp(query_cot, d) for d in (1, 2, 3)]
    partial_grad = jnp.dot(
        inputs,
        jnp.concatenate(cots, axis=0),
        preferred_element_type=jnp.float32,
    )
    partial_grad = partial_grad.astype(jnp.bfloat16).reshape(mem_count, -1, 2 * half)
    spread = lax.all_to_all(partial_grad, "mem", 0, 0, tiled=True)
    query_grad = jnp.sum(spread.astype(jnp.float32), axis=0)

    left_y = ring_sum(left_x.reshape(Y, -1, cols), along_y)
    right_x = ring_sum(right_y.reshape(dp_count, -1, cols), shift_dp)
    value_grad = jnp.concatenate(
        [left_y.astype(jnp.bfloat16), right_x.astype(jnp.bfloat16)], axis=1
    )

    input_grad = lax.dot_general(query_cot, weight, NT, preferred_element_type=jnp.float32)
    handed = lax.ppermute(input_grad.astype(jnp.bfloat16), "section", [(0, 1), (1, 0)])
    return (value_grad[None], query_grad[None], handed[None])


def solution(mesh):
    placed = (
        P("section", ("mem", "dp"), None),
        P("section", ("mem", "dp"), None),
        P("section", None, None),
        P("section", None, None),
        P("section", None, None),
        P("section", "mem", None),
        P("section", None, None),
    )
    return jax.shard_map(
        shards,
        mesh=mesh,
        in_specs=placed,
        out_specs=(
            P("section", ("mem", "dp"), None),
            P("section", ("mem", "dp"), None),
            P("section", ("mem", "dp"), None),
        ),
        check_vma=False,
    )
```

```python
import functools
import math

import jax
import jax.numpy as jnp
from jax import lax
from jax.experimental import pallas as pl
from jax.experimental.pallas import tpu as pltpu
from jax.sharding import PartitionSpec as P

EPS = 1e-06
HIGHEST = lax.Precision.HIGHEST
VMEM = pl.BlockSpec(memory_space=pltpu.VMEM)
SMEM = pl.BlockSpec(memory_space=pltpu.SMEM)
NT = (((1,), (1,)), ((), ()))
Y = 4
TAIL = 16
LANES = 128


def shift_mem(block, dz, dy):
    count = lax.axis_size("mem")
    depth = count // Y
    route = []
    for z in range(depth):
        for y in range(Y):
            route.append((z * Y + y, ((z + dz) % depth) * Y + (y + dy) % Y))
    return lax.ppermute(block, "mem", route)


def shift_dp(block, step):
    count = lax.axis_size("dp")
    return lax.ppermute(block, "dp", [(i, (i + step) % count) for i in range(count)])


def normed(part):
    scale = lax.rsqrt(jnp.mean(part * part, axis=0, keepdims=True) + EPS)
    return part * scale, scale


def head_kernel(ids, x_ref, w_ref, k1_ref, k2_ref, up_ref, probs_ref, q_ref, keys_ref, load_ref):
    picks, half = keys_ref.shape
    q = jnp.dot(x_ref[...], w_ref[...], preferred_element_type=jnp.float32)
    q = q.astype(jnp.bfloat16).astype(jnp.float32)
    q_t = q.T
    q_ref[...] = q_t
    for k in range(picks):
        keys_ref[k : k + 1, :] = k1_ref[pl.ds(ids[k], 1), :]
    factor = 1.0 / math.sqrt(half)
    first, _ = normed(q_t[:half])
    second, _ = normed(q_t[half:])
    block_exp = jnp.exp(
        jnp.dot(keys_ref[...], first, precision=HIGHEST, preferred_element_type=jnp.float32) * factor
    )
    row_exp = jnp.exp(
        jnp.dot(k2_ref[...], second, precision=HIGHEST, preferred_element_type=jnp.float32) * factor
    )
    probs_ref[:picks, :] = block_exp / jnp.sum(block_exp, axis=0, keepdims=True)
    probs_ref[picks:, :] = row_exp / jnp.sum(row_exp, axis=0, keepdims=True)
    tokens = up_ref.shape[0]
    load_ref[:tokens, :] = up_ref[...]
    load_ref[tokens:, :] = jnp.zeros((TAIL, up_ref.shape[1]), jnp.bfloat16)
    tiles = probs_ref.shape[0] // TAIL
    for i in range(tiles):
        tile = probs_ref[i * TAIL : (i + 1) * TAIL, :]
        high = tile.astype(jnp.bfloat16)
        low = (tile - high.astype(jnp.float32)).astype(jnp.bfloat16)
        load_ref[tokens:, i * LANES : (i + 1) * LANES] = high
        load_ref[tokens:, (tiles + i) * LANES : (tiles + i + 1) * LANES] = low


def tail_kernel(source, place, recv_ref, probs_ref, q_ref, keys_ref, k2_ref, out_ref, cot_ref):
    picks, half = keys_ref.shape
    rows = k2_ref.shape[0]
    factor = 1.0 / math.sqrt(half)
    row_cot = jnp.sum(recv_ref[:, :rows, :], axis=0)
    for k in range(picks):
        cot_ref[k : k + 1, :] = recv_ref[source[k], pl.ds(rows + place[k], 1), :]
    block_cot = cot_ref[...]
    q_t = q_ref[...]

    def through(part, probs, cot, keys):
        unit, scale = normed(part)
        logit_cot = probs * (cot - jnp.sum(probs * cot, axis=0, keepdims=True)) * factor
        unit_cot = jnp.dot(
            keys.T, logit_cot, precision=HIGHEST, preferred_element_type=jnp.float32
        )
        inner = jnp.mean(unit * unit_cot, axis=0, keepdims=True)
        return scale * (unit_cot - unit * inner)

    lead = through(q_t[:half], probs_ref[:picks, :], block_cot, keys_ref[...])
    trail = through(q_t[half:], probs_ref[picks:, :], row_cot, k2_ref[...])
    out_ref[:, :half] = lead.T.astype(jnp.bfloat16)
    out_ref[:, half:] = trail.T.astype(jnp.bfloat16)


def table_kernel(chosen_ref, low_ref, rp_ref, *slot_refs):
    picks = chosen_ref.shape[2]
    tiles = (picks + rp_ref.shape[1]) // TAIL
    each = slot_refs[0].shape[1]
    for g in range(low_ref.shape[0]):

        def tile(i):
            high = low_ref[g, :, i * LANES : (i + 1) * LANES].astype(jnp.float32)
            rest = low_ref[g, :, (tiles + i) * LANES : (tiles + i + 1) * LANES]
            return high + rest.astype(jnp.float32)

        first = picks // TAIL
        block_probs = jnp.concatenate([tile(i) for i in range(first)], axis=0)
        for i in range(first, tiles):
            rp_ref[g, (i - first) * TAIL : (i - first + 1) * TAIL, :] = tile(i)
        slots = jnp.dot(
            chosen_ref[g], block_probs, precision=HIGHEST, preferred_element_type=jnp.float32
        )
        for n, ref in enumerate(slot_refs):
            ref[g] = slots[n * each : (n + 1) * each]


def return_kernel(up_ref, rp_ref, sp_ref, v_ref, out_ref, flat_ref):
    groups, rows, group_rows = rp_ref.shape
    blocks = sp_ref.shape[1]
    step = pl.program_id(0)

    @pl.when(step == 0)
    def _():
        for g in range(groups):
            flat_ref[g * group_rows : (g + 1) * group_rows, :] = up_ref[g, :group_rows, :]
            out_ref[g, :rows, :] = jnp.zeros((rows, group_rows), jnp.float32)

    products = lax.dot_general(v_ref[...], flat_ref[...], NT, preferred_element_type=jnp.float32)
    slots = pl.ds(pl.multiple_of(rows + step * blocks, blocks), blocks)
    for g in range(groups):
        row_probs = rp_ref[g]
        total = out_ref[g, :rows, :]
        sums = []
        for b in range(blocks):
            part = products[b * rows : (b + 1) * rows, g * group_rows : (g + 1) * group_rows]
            total = total + part * sp_ref[g, b : b + 1, :]
            sums.append(jnp.sum(part * row_probs, axis=0, keepdims=True))
        out_ref[g, :rows, :] = total
        out_ref[g, slots, :] = jnp.concatenate(sums, axis=0)


def cotangents(up, row_probs, slot_probs, held):
    groups, rows, group_rows = row_probs.shape
    slots = slot_probs.shape[1]
    width = up.shape[2]
    each = 8
    return pl.pallas_call(
        return_kernel,
        out_shape=jax.ShapeDtypeStruct((groups, rows + slots, group_rows), jnp.float32),
        grid=(slots // each,),
        in_specs=[
            pl.BlockSpec(up.shape, lambda i: (0, 0, 0)),
            pl.BlockSpec(row_probs.shape, lambda i: (0, 0, 0)),
            pl.BlockSpec((groups, each, group_rows), lambda i: (0, i, 0)),
            pl.BlockSpec((each * rows, width), lambda i: (i, 0)),
        ],
        out_specs=pl.BlockSpec((groups, rows + slots, group_rows), lambda i: (0, 0, 0)),
        scratch_shapes=[pltpu.VMEM((groups * group_rows, width), jnp.bfloat16)],
        compiler_params=pltpu.CompilerParams(vmem_limit_bytes=40 * 1024 * 1024),
        cost_estimate=pl.CostEstimate(
            flops=2 * groups * group_rows * slots * rows * width,
            bytes_accessed=2 * (groups * group_rows + slots * rows) * width,
            transcendentals=0,
        ),
        name="returns",
    )(up, row_probs, slot_probs, held)


def sum_kernel(rows, rp_ref, sp_ref, up_ref, out_ref, tile_ref, flat_ref):
    groups = rp_ref.shape[0]
    group_rows = rp_ref.shape[2]

    @pl.when(pl.program_id(0) == 0)
    def _():
        for g in range(groups):
            flat_ref[g * group_rows : (g + 1) * group_rows, :] = up_ref[g, :group_rows, :]

    for g in range(groups):
        row_probs = rp_ref[g]
        for b in range(sp_ref.shape[1]):
            tile_ref[b * rows : (b + 1) * rows, g * group_rows : (g + 1) * group_rows] = (
                sp_ref[g, b : b + 1, :] * row_probs
            ).astype(jnp.bfloat16)
    out_ref[...] = jnp.dot(
        tile_ref[...], flat_ref[...], preferred_element_type=jnp.float32
    ).astype(jnp.bfloat16)


def value_sums(row_probs, slot_probs, up, part):
    groups, rows, group_rows = row_probs.shape
    blocks = slot_probs.shape[1]
    tokens = groups * group_rows
    cols = up.shape[2] // 2
    each = 8
    return pl.pallas_call(
        functools.partial(sum_kernel, rows),
        out_shape=jax.ShapeDtypeStruct((blocks * rows, cols), jnp.bfloat16),
        grid=(blocks // each,),
        in_specs=[
            pl.BlockSpec((groups, rows, group_rows), lambda i: (0, 0, 0)),
            pl.BlockSpec((groups, each, group_rows), lambda i: (0, i, 0)),
            pl.BlockSpec((groups, up.shape[1], cols), lambda i: (0, 0, part)),
        ],
        out_specs=pl.BlockSpec((each * rows, cols), lambda i: (i, 0)),
        scratch_shapes=[
            pltpu.VMEM((each * rows, tokens), jnp.bfloat16),
            pltpu.VMEM((tokens, cols), jnp.bfloat16),
        ],
        compiler_params=pltpu.CompilerParams(vmem_limit_bytes=32 * 1024 * 1024),
        cost_estimate=pl.CostEstimate(
            flops=2 * blocks * rows * tokens * cols,
            bytes_accessed=2 * (tokens * cols + blocks * rows * cols),
            transcendentals=0,
        ),
        name="value_sums",
    )(row_probs, slot_probs, up)


def ring_gather(block, shift):
    low = shift(block, 1)
    high = shift(block, -1)
    cut = block.shape[0] // 2
    far = (shift(low[:cut], 1), shift(high[cut:], -1))
    return low, high, far


def wide(a):
    return a.astype(jnp.float32)


def ring_far(parts, shift):
    cut = parts.shape[1] // 2
    return shift(parts[2, :cut], 1), shift(parts[2, cut:], -1)


def ring_mix(parts, far):
    cut = parts.shape[1] // 2
    up = jnp.concatenate(
        [(wide(parts[1, :cut]) + wide(far[0])).astype(jnp.bfloat16), parts[1, cut:]], axis=0
    )
    down = jnp.concatenate(
        [parts[3, :cut], (wide(parts[3, cut:]) + wide(far[1])).astype(jnp.bfloat16)], axis=0
    )
    return up, down


def ring_end(parts, mixed, shift):
    return wide(parts[0]) + wide(shift(mixed[0], 1)) + wide(shift(mixed[1], -1))


def ring_sum(parts, shift):
    return ring_end(parts, ring_mix(parts, ring_far(parts, shift)), shift)


def shards(layer_input, out_grad, query_weight, key_one, key_two, values, block_ids):
    tokens = layer_input[0]
    upstream = out_grad[0]
    weight = query_weight[0]
    first_table = key_one[0]
    second_table = key_two[0]
    all_ids = block_ids[0]
    group_rows, width = tokens.shape
    half = weight.shape[1] // 2
    rows = second_table.shape[0]
    per_owner = values.shape[1] // rows
    picks = all_ids.shape[1]
    mem_count = lax.axis_size("mem")
    dp_count = lax.axis_size("dp")
    depth = mem_count // Y
    mem_index = lax.axis_index("mem")
    dp_index = lax.axis_index("dp")
    z_index = mem_index // Y
    y_index = mem_index % Y
    own_ids = lax.dynamic_index_in_dim(all_ids, mem_index * dp_count + dp_index, 0, keepdims=False)
    cols = width // 2
    line = [[z * Y + y for z in range(depth)] for y in range(Y)]
    along_y = lambda block, step: shift_mem(block, 0, step)


    own_values = values[0]
    direct_rows = 4 * rows
    one_block = lax.dynamic_slice_in_dim(own_values, direct_rows + dp_index * rows, rows, 0)
    one_block, tokens = lax.optimization_barrier((one_block, tokens))
    low_b, high_b, far_b = ring_gather(one_block, along_y)
    direct, far_b = lax.optimization_barrier((own_values[:direct_rows], far_b))
    low_d = along_y(direct, 1)
    high_d = along_y(direct, -1)
    spread_x = jnp.concatenate([low_b, high_b, *far_b], axis=0)

    probs, q_t, own_keys, load = pl.pallas_call(
        head_kernel,
        out_shape=(
            jax.ShapeDtypeStruct((picks + rows, group_rows), jnp.float32),
            jax.ShapeDtypeStruct((2 * half, group_rows), jnp.float32),
            jax.ShapeDtypeStruct((picks, half), jnp.float32),
            jax.ShapeDtypeStruct((group_rows + TAIL, width), jnp.bfloat16),
        ),
        in_specs=[SMEM] + [VMEM] * 5,
        out_specs=(VMEM,) * 4,
        compiler_params=pltpu.CompilerParams(vmem_limit_bytes=24 * 1024 * 1024),
        name="head",
    )(own_ids, tokens, weight, first_table, second_table, upstream)

    gathered = lax.all_gather(load, "mem", axis=0, axis_index_groups=line)

    cut = direct_rows // 2
    far_d = (along_y(low_d[:cut], 1), along_y(high_d[cut:], -1))
    low_x = shift_dp(spread_x, 1)
    high_x = shift_dp(spread_x, -1)
    late_tokens, low_x, high_x = lax.optimization_barrier((tokens, low_x, high_x))
    cut = spread_x.shape[0] // 2
    far_x = (shift_dp(low_x[:cut], 1), shift_dp(high_x[cut:], -1))

    y_at = (y_index + jnp.arange(Y)) % Y
    x_at = (dp_index + jnp.arange(dp_count)) % dp_count
    shard_base = (z_index * Y + y_at) * per_owner
    per_x = per_owner // dp_count
    x_blocks = x_at[:, None] * per_x + jnp.arange(per_x)[None, :]
    y_first = (shard_base[:, None, None] + x_blocks[None, :, :]).reshape(-1)
    x_first = (shard_base[None, :, None] + x_blocks[:, None, :]).reshape(-1)
    octets = shard_base[jnp.array([3, 1, 2])]
    x_held = x_at[jnp.array([0, 3, 1, 2])]
    held = jnp.concatenate(
        [
            shard_base[0] + jnp.arange(per_owner),
            (octets[:, None] + jnp.arange(4)[None, :]).reshape(-1),
            (octets[None, :] + 4 + x_held[:, None]).reshape(-1),
        ]
    )
    wanted = jnp.concatenate([held, x_first, y_first])
    cells = all_ids.reshape(depth, Y * dp_count, picks)
    line_ids = lax.dynamic_index_in_dim(cells, y_index * dp_count + dp_index, 1, keepdims=False)
    chosen = (line_ids[:, None, :] == wanted[None, :, None]).astype(jnp.float32)
    count = Y * per_owner
    slots = jax.ShapeDtypeStruct((depth, count, group_rows), jnp.float32)
    row_probs, held_probs, left_probs, right_probs = pl.pallas_call(
        table_kernel,
        out_shape=(jax.ShapeDtypeStruct((depth, rows, group_rows), jnp.float32),) + (slots,) * 3,
        grid=(1,),
        in_specs=[
            pl.BlockSpec(chosen.shape, lambda i: (0, 0, 0)),
            pl.BlockSpec((depth, TAIL, width), lambda i: (0, group_rows // TAIL, 0)),
        ],
        out_specs=(
            pl.BlockSpec((depth, rows, group_rows), lambda i: (0, 0, 0)),
        )
        + (pl.BlockSpec(slots.shape, lambda i: (0, 0, 0)),) * 3,
        name="tables",
    )(chosen, gathered)
    left_sums = value_sums(row_probs, left_probs, gathered, 0)
    right_sums = value_sums(row_probs, right_probs, gathered, 1)

    turned = late_tokens.T.reshape(mem_count, dp_count, width // (mem_count * dp_count), group_rows)
    turned = turned.transpose(1, 0, 2, 3).reshape(dp_count, width // dp_count, group_rows)

    def piece(offset):
        return lax.dynamic_index_in_dim(turned, (dp_index + offset) % dp_count, 0, keepdims=False)

    inputs = [piece(0)] + [shift_dp(piece(d), d) for d in (1, 2, 3)]
    inputs = jnp.concatenate(inputs, axis=1)
    left_parts = left_sums.reshape(dp_count, -1, cols)
    right_parts = right_sums.reshape(Y, -1, cols)
    left_far = ring_far(left_parts, shift_dp)
    right_far = ring_far(right_parts, along_y)
    left_mixed = ring_mix(left_parts, left_far)
    held_probs, inputs, left_mixed = lax.optimization_barrier((held_probs, inputs, left_mixed))
    left_sums, far_d, far_x = lax.optimization_barrier((left_sums, far_d, far_x))
    held_values = jnp.concatenate(
        [own_values, low_d, high_d, *far_d, spread_x, low_x, high_x, *far_x], axis=0
    )
    returned = cotangents(gathered, row_probs, held_probs, held_values)

    received = lax.all_to_all(returned, "mem", 0, 0, tiled=True, axis_index_groups=line)
    source = own_ids // count
    dy = (own_ids // per_owner - y_index + Y) % Y
    inside = own_ids % per_owner
    octet = jnp.array([0, 1, 2, 0])[dy]
    x_slot = jnp.array([0, 2, 3, 1])[(inside - 4 - dp_index + 2 * dp_count) % dp_count]
    place = jnp.where(
        dy == 0,
        inside,
        jnp.where(inside < 4, per_owner + octet * 4 + inside, per_owner + 12 + x_slot * 3 + octet),
    )
    left_x = ring_end(left_parts, left_mixed, shift_dp).astype(jnp.bfloat16)
    right_mixed = ring_mix(right_parts, right_far)
    right_y = ring_end(right_parts, right_mixed, along_y).astype(jnp.bfloat16)
    received, left_x, right_y = lax.optimization_barrier((received, left_x, right_y))
    query_cot = pl.pallas_call(
        tail_kernel,
        out_shape=jax.ShapeDtypeStruct((group_rows, 2 * half), jnp.bfloat16),
        in_specs=[SMEM, SMEM] + [VMEM] * 5,
        out_specs=VMEM,
        scratch_shapes=[pltpu.VMEM((picks, group_rows), jnp.float32)],
        compiler_params=pltpu.CompilerParams(vmem_limit_bytes=24 * 1024 * 1024),
        name="tail",
    )(source, place, received, probs, q_t, own_keys, second_table)

    cots = [query_cot] + [shift_dp(query_cot, d) for d in (1, 2, 3)]
    partial_grad = jnp.dot(
        inputs,
        jnp.concatenate(cots, axis=0),
        preferred_element_type=jnp.float32,
    )
    partial_grad = partial_grad.astype(jnp.bfloat16).reshape(mem_count, -1, 2 * half)
    spread = lax.all_to_all(partial_grad, "mem", 0, 0, tiled=True)
    query_grad = jnp.sum(spread.astype(jnp.float32), axis=0)

    left_y = ring_sum(left_x.reshape(Y, -1, cols), along_y)
    right_x = ring_sum(right_y.reshape(dp_count, -1, cols), shift_dp)
    value_grad = jnp.concatenate(
        [left_y.astype(jnp.bfloat16), right_x.astype(jnp.bfloat16)], axis=1
    )

    input_grad = lax.dot_general(query_cot, weight, NT, preferred_element_type=jnp.float32)
    handed = lax.ppermute(input_grad.astype(jnp.bfloat16), "section", [(0, 1), (1, 0)])
    return (value_grad[None], query_grad[None], handed[None])


def solution(mesh):
    placed = (
        P("section", ("mem", "dp"), None),
        P("section", ("mem", "dp"), None),
        P("section", None, None),
        P("section", None, None),
        P("section", None, None),
        P("section", "mem", None),
        P("section", None, None),
    )
    return jax.shard_map(
        shards,
        mesh=mesh,
        in_specs=placed,
        out_specs=(
            P("section", ("mem", "dp"), None),
            P("section", ("mem", "dp"), None),
            P("section", ("mem", "dp"), None),
        ),
        check_vma=False,
    )
```

```python
import functools
import math

import jax
import jax.numpy as jnp
from jax import lax
from jax.experimental import pallas as pl
from jax.experimental.pallas import tpu as pltpu
from jax.sharding import PartitionSpec as P

EPS = 1e-06
HIGHEST = lax.Precision.HIGHEST
VMEM = pl.BlockSpec(memory_space=pltpu.VMEM)
SMEM = pl.BlockSpec(memory_space=pltpu.SMEM)
NT = (((1,), (1,)), ((), ()))
Y = 4
TAIL = 16
LANES = 128


def shift_mem(block, dz, dy):
    count = lax.axis_size("mem")
    depth = count // Y
    route = []
    for z in range(depth):
        for y in range(Y):
            route.append((z * Y + y, ((z + dz) % depth) * Y + (y + dy) % Y))
    return lax.ppermute(block, "mem", route)


def shift_dp(block, step):
    count = lax.axis_size("dp")
    return lax.ppermute(block, "dp", [(i, (i + step) % count) for i in range(count)])


def normed(part):
    scale = lax.rsqrt(jnp.mean(part * part, axis=0, keepdims=True) + EPS)
    return part * scale, scale


def head_kernel(ids, x_ref, w_ref, k1_ref, k2_ref, up_ref, probs_ref, q_ref, keys_ref, load_ref):
    picks, half = keys_ref.shape
    q = jnp.dot(x_ref[...], w_ref[...], preferred_element_type=jnp.float32)
    q = q.astype(jnp.bfloat16).astype(jnp.float32)
    q_t = q.T
    q_ref[...] = q_t
    for k in range(picks):
        keys_ref[k : k + 1, :] = k1_ref[pl.ds(ids[k], 1), :]
    factor = 1.0 / math.sqrt(half)
    first, _ = normed(q_t[:half])
    second, _ = normed(q_t[half:])
    block_exp = jnp.exp(
        jnp.dot(keys_ref[...], first, precision=HIGHEST, preferred_element_type=jnp.float32) * factor
    )
    row_exp = jnp.exp(
        jnp.dot(k2_ref[...], second, precision=HIGHEST, preferred_element_type=jnp.float32) * factor
    )
    probs_ref[:picks, :] = block_exp / jnp.sum(block_exp, axis=0, keepdims=True)
    probs_ref[picks:, :] = row_exp / jnp.sum(row_exp, axis=0, keepdims=True)
    tokens = up_ref.shape[0]
    load_ref[:tokens, :] = up_ref[...]
    load_ref[tokens:, :] = jnp.zeros((TAIL, up_ref.shape[1]), jnp.bfloat16)
    tiles = probs_ref.shape[0] // TAIL
    for i in range(tiles):
        tile = probs_ref[i * TAIL : (i + 1) * TAIL, :]
        high = tile.astype(jnp.bfloat16)
        low = (tile - high.astype(jnp.float32)).astype(jnp.bfloat16)
        load_ref[tokens:, i * LANES : (i + 1) * LANES] = high
        load_ref[tokens:, (tiles + i) * LANES : (tiles + i + 1) * LANES] = low


def tail_kernel(source, place, recv_ref, probs_ref, q_ref, keys_ref, k2_ref, out_ref, cot_ref):
    picks, half = keys_ref.shape
    rows = k2_ref.shape[0]
    factor = 1.0 / math.sqrt(half)
    row_cot = jnp.sum(recv_ref[:, :rows, :], axis=0)
    for k in range(picks):
        cot_ref[k : k + 1, :] = recv_ref[source[k], pl.ds(rows + place[k], 1), :]
    block_cot = cot_ref[...]
    q_t = q_ref[...]

    def through(part, probs, cot, keys):
        unit, scale = normed(part)
        logit_cot = probs * (cot - jnp.sum(probs * cot, axis=0, keepdims=True)) * factor
        unit_cot = jnp.dot(
            keys.T, logit_cot, precision=HIGHEST, preferred_element_type=jnp.float32
        )
        inner = jnp.mean(unit * unit_cot, axis=0, keepdims=True)
        return scale * (unit_cot - unit * inner)

    lead = through(q_t[:half], probs_ref[:picks, :], block_cot, keys_ref[...])
    trail = through(q_t[half:], probs_ref[picks:, :], row_cot, k2_ref[...])
    out_ref[:, :half] = lead.T.astype(jnp.bfloat16)
    out_ref[:, half:] = trail.T.astype(jnp.bfloat16)


def table_kernel(chosen_ref, low_ref, rp_ref, *slot_refs):
    picks = chosen_ref.shape[2]
    tiles = (picks + rp_ref.shape[1]) // TAIL
    each = slot_refs[0].shape[1]
    for g in range(low_ref.shape[0]):

        def tile(i):
            high = low_ref[g, :, i * LANES : (i + 1) * LANES].astype(jnp.float32)
            rest = low_ref[g, :, (tiles + i) * LANES : (tiles + i + 1) * LANES]
            return high + rest.astype(jnp.float32)

        first = picks // TAIL
        block_probs = jnp.concatenate([tile(i) for i in range(first)], axis=0)
        for i in range(first, tiles):
            rp_ref[g, (i - first) * TAIL : (i - first + 1) * TAIL, :] = tile(i)
        slots = jnp.dot(
            chosen_ref[g], block_probs, precision=HIGHEST, preferred_element_type=jnp.float32
        )
        for n, ref in enumerate(slot_refs):
            ref[g] = slots[n * each : (n + 1) * each]


def return_kernel(up_ref, rp_ref, sp_ref, v_ref, out_ref, flat_ref):
    groups, rows, group_rows = rp_ref.shape
    blocks = sp_ref.shape[1]
    step = pl.program_id(0)

    @pl.when(step == 0)
    def _():
        for g in range(groups):
            flat_ref[g * group_rows : (g + 1) * group_rows, :] = up_ref[g, :group_rows, :]
            out_ref[g, :rows, :] = jnp.zeros((rows, group_rows), jnp.float32)

    products = lax.dot_general(v_ref[...], flat_ref[...], NT, preferred_element_type=jnp.float32)
    slots = pl.ds(pl.multiple_of(rows + step * blocks, blocks), blocks)
    for g in range(groups):
        row_probs = rp_ref[g]
        total = out_ref[g, :rows, :]
        sums = []
        for b in range(blocks):
            part = products[b * rows : (b + 1) * rows, g * group_rows : (g + 1) * group_rows]
            total = total + part * sp_ref[g, b : b + 1, :]
            sums.append(jnp.sum(part * row_probs, axis=0, keepdims=True))
        out_ref[g, :rows, :] = total
        out_ref[g, slots, :] = jnp.concatenate(sums, axis=0)


def cotangents(up, row_probs, slot_probs, held):
    groups, rows, group_rows = row_probs.shape
    slots = slot_probs.shape[1]
    width = up.shape[2]
    each = 8
    return pl.pallas_call(
        return_kernel,
        out_shape=jax.ShapeDtypeStruct((groups, rows + slots, group_rows), jnp.float32),
        grid=(slots // each,),
        in_specs=[
            pl.BlockSpec(up.shape, lambda i: (0, 0, 0)),
            pl.BlockSpec(row_probs.shape, lambda i: (0, 0, 0)),
            pl.BlockSpec((groups, each, group_rows), lambda i: (0, i, 0)),
            pl.BlockSpec((each * rows, width), lambda i: (i, 0)),
        ],
        out_specs=pl.BlockSpec((groups, rows + slots, group_rows), lambda i: (0, 0, 0)),
        scratch_shapes=[pltpu.VMEM((groups * group_rows, width), jnp.bfloat16)],
        compiler_params=pltpu.CompilerParams(vmem_limit_bytes=40 * 1024 * 1024),
        cost_estimate=pl.CostEstimate(
            flops=2 * groups * group_rows * slots * rows * width,
            bytes_accessed=2 * (groups * group_rows + slots * rows) * width,
            transcendentals=0,
        ),
        name="returns",
    )(up, row_probs, slot_probs, held)


def sum_kernel(rows, rp_ref, sp_ref, up_ref, out_ref, tile_ref, flat_ref):
    groups = rp_ref.shape[0]
    group_rows = rp_ref.shape[2]

    @pl.when(pl.program_id(0) == 0)
    def _():
        for g in range(groups):
            flat_ref[g * group_rows : (g + 1) * group_rows, :] = up_ref[g, :group_rows, :]

    for g in range(groups):
        row_probs = rp_ref[g]
        for b in range(sp_ref.shape[1]):
            tile_ref[b * rows : (b + 1) * rows, g * group_rows : (g + 1) * group_rows] = (
                sp_ref[g, b : b + 1, :] * row_probs
            ).astype(jnp.bfloat16)
    out_ref[...] = jnp.dot(
        tile_ref[...], flat_ref[...], preferred_element_type=jnp.float32
    ).astype(jnp.bfloat16)


def value_sums(row_probs, slot_probs, up, part):
    groups, rows, group_rows = row_probs.shape
    blocks = slot_probs.shape[1]
    tokens = groups * group_rows
    cols = up.shape[2] // 2
    each = 8
    return pl.pallas_call(
        functools.partial(sum_kernel, rows),
        out_shape=jax.ShapeDtypeStruct((blocks * rows, cols), jnp.bfloat16),
        grid=(blocks // each,),
        in_specs=[
            pl.BlockSpec((groups, rows, group_rows), lambda i: (0, 0, 0)),
            pl.BlockSpec((groups, each, group_rows), lambda i: (0, i, 0)),
            pl.BlockSpec((groups, up.shape[1], cols), lambda i: (0, 0, part)),
        ],
        out_specs=pl.BlockSpec((each * rows, cols), lambda i: (i, 0)),
        scratch_shapes=[
            pltpu.VMEM((each * rows, tokens), jnp.bfloat16),
            pltpu.VMEM((tokens, cols), jnp.bfloat16),
        ],
        compiler_params=pltpu.CompilerParams(vmem_limit_bytes=56 * 1024 * 1024),
        cost_estimate=pl.CostEstimate(
            flops=2 * blocks * rows * tokens * cols,
            bytes_accessed=2 * (tokens * cols + blocks * rows * cols),
            transcendentals=0,
        ),
        name="value_sums",
    )(row_probs, slot_probs, up)


def ring_gather(block, shift):
    low = shift(block, 1)
    high = shift(block, -1)
    cut = block.shape[0] // 2
    far = (shift(low[:cut], 1), shift(high[cut:], -1))
    return low, high, far


def wide(a):
    return a.astype(jnp.float32)


def ring_far(parts, shift):
    cut = parts.shape[1] // 2
    return shift(parts[2, :cut], 1), shift(parts[2, cut:], -1)


def ring_mix(parts, far):
    cut = parts.shape[1] // 2
    up = jnp.concatenate(
        [(wide(parts[1, :cut]) + wide(far[0])).astype(jnp.bfloat16), parts[1, cut:]], axis=0
    )
    down = jnp.concatenate(
        [parts[3, :cut], (wide(parts[3, cut:]) + wide(far[1])).astype(jnp.bfloat16)], axis=0
    )
    return up, down


def ring_near(mixed, shift):
    return shift(mixed[0], 1), shift(mixed[1], -1)


def ring_end(parts, near):
    return wide(parts[0]) + wide(near[0]) + wide(near[1])


def ring_sum(parts, shift):
    return ring_end(parts, ring_near(ring_mix(parts, ring_far(parts, shift)), shift))


def shards(layer_input, out_grad, query_weight, key_one, key_two, values, block_ids):
    tokens = layer_input[0]
    upstream = out_grad[0]
    weight = query_weight[0]
    first_table = key_one[0]
    second_table = key_two[0]
    all_ids = block_ids[0]
    group_rows, width = tokens.shape
    half = weight.shape[1] // 2
    rows = second_table.shape[0]
    per_owner = values.shape[1] // rows
    picks = all_ids.shape[1]
    mem_count = lax.axis_size("mem")
    dp_count = lax.axis_size("dp")
    depth = mem_count // Y
    mem_index = lax.axis_index("mem")
    dp_index = lax.axis_index("dp")
    z_index = mem_index // Y
    y_index = mem_index % Y
    own_ids = lax.dynamic_index_in_dim(all_ids, mem_index * dp_count + dp_index, 0, keepdims=False)
    cols = width // 2
    line = [[z * Y + y for z in range(depth)] for y in range(Y)]
    along_y = lambda block, step: shift_mem(block, 0, step)


    own_values = values[0]
    direct_rows = 4 * rows
    one_block = lax.dynamic_slice_in_dim(own_values, direct_rows + dp_index * rows, rows, 0)
    low_b, high_b, far_b = ring_gather(one_block, along_y)
    direct, far_b = lax.optimization_barrier((own_values[:direct_rows], far_b))
    low_d = along_y(direct, 1)
    high_d = along_y(direct, -1)
    spread_x = jnp.concatenate([low_b, high_b, *far_b], axis=0)

    probs, q_t, own_keys, load = pl.pallas_call(
        head_kernel,
        out_shape=(
            jax.ShapeDtypeStruct((picks + rows, group_rows), jnp.float32),
            jax.ShapeDtypeStruct((2 * half, group_rows), jnp.float32),
            jax.ShapeDtypeStruct((picks, half), jnp.float32),
            jax.ShapeDtypeStruct((group_rows + TAIL, width), jnp.bfloat16),
        ),
        in_specs=[SMEM] + [VMEM] * 5,
        out_specs=(VMEM,) * 4,
        compiler_params=pltpu.CompilerParams(vmem_limit_bytes=56 * 1024 * 1024),
        name="head",
    )(own_ids, tokens, weight, first_table, second_table, upstream)

    gathered = lax.all_gather(load, "mem", axis=0, axis_index_groups=line)

    cut = direct_rows // 2
    far_d = (along_y(low_d[:cut], 1), along_y(high_d[cut:], -1))
    low_x = shift_dp(spread_x, 1)
    high_x = shift_dp(spread_x, -1)
    late_tokens, low_x, high_x = lax.optimization_barrier((tokens, low_x, high_x))
    cut = spread_x.shape[0] // 2
    far_x = (shift_dp(low_x[:cut], 1), shift_dp(high_x[cut:], -1))

    y_at = (y_index + jnp.arange(Y)) % Y
    x_at = (dp_index + jnp.arange(dp_count)) % dp_count
    shard_base = (z_index * Y + y_at) * per_owner
    per_x = per_owner // dp_count
    x_blocks = x_at[:, None] * per_x + jnp.arange(per_x)[None, :]
    y_first = (shard_base[:, None, None] + x_blocks[None, :, :]).reshape(-1)
    x_first = (shard_base[None, :, None] + x_blocks[:, None, :]).reshape(-1)
    octets = shard_base[jnp.array([3, 1, 2])]
    x_held = x_at[jnp.array([0, 3, 1, 2])]
    held = jnp.concatenate(
        [
            shard_base[0] + jnp.arange(per_owner),
            (octets[:, None] + jnp.arange(4)[None, :]).reshape(-1),
            (octets[None, :] + 4 + x_held[:, None]).reshape(-1),
        ]
    )
    wanted = jnp.concatenate([held, x_first, y_first])
    cells = all_ids.reshape(depth, Y * dp_count, picks)
    line_ids = lax.dynamic_index_in_dim(cells, y_index * dp_count + dp_index, 1, keepdims=False)
    chosen = (line_ids[:, None, :] == wanted[None, :, None]).astype(jnp.float32)
    count = Y * per_owner
    slots = jax.ShapeDtypeStruct((depth, count, group_rows), jnp.float32)
    row_probs, held_probs, left_probs, right_probs = pl.pallas_call(
        table_kernel,
        out_shape=(jax.ShapeDtypeStruct((depth, rows, group_rows), jnp.float32),) + (slots,) * 3,
        grid=(1,),
        in_specs=[
            pl.BlockSpec(chosen.shape, lambda i: (0, 0, 0)),
            pl.BlockSpec((depth, TAIL, width), lambda i: (0, group_rows // TAIL, 0)),
        ],
        out_specs=(
            pl.BlockSpec((depth, rows, group_rows), lambda i: (0, 0, 0)),
        )
        + (pl.BlockSpec(slots.shape, lambda i: (0, 0, 0)),) * 3,
        compiler_params=pltpu.CompilerParams(vmem_limit_bytes=56 * 1024 * 1024),
        name="tables",
    )(chosen, gathered)
    left_sums = value_sums(row_probs, left_probs, gathered, 0)
    right_sums = value_sums(row_probs, right_probs, gathered, 1)

    turned = late_tokens.T.reshape(mem_count, dp_count, width // (mem_count * dp_count), group_rows)
    turned = turned.transpose(1, 0, 2, 3).reshape(dp_count, width // dp_count, group_rows)

    def piece(offset):
        return lax.dynamic_index_in_dim(turned, (dp_index + offset) % dp_count, 0, keepdims=False)

    inputs = [piece(0)] + [shift_dp(piece(d), d) for d in (1, 2, 3)]
    inputs = jnp.concatenate(inputs, axis=1)
    left_parts = left_sums.reshape(dp_count, -1, cols)
    right_parts = right_sums.reshape(Y, -1, cols)
    left_far = ring_far(left_parts, shift_dp)
    right_far = ring_far(right_parts, along_y)
    left_mixed = ring_mix(left_parts, left_far)
    held_probs, inputs, left_mixed = lax.optimization_barrier((held_probs, inputs, left_mixed))
    left_sums, far_d, far_x = lax.optimization_barrier((left_sums, far_d, far_x))
    held_values = jnp.concatenate(
        [own_values, low_d, high_d, *far_d, spread_x, low_x, high_x, *far_x], axis=0
    )
    returned = cotangents(gathered, row_probs, held_probs, held_values)

    received = lax.all_to_all(returned, "mem", 0, 0, tiled=True, axis_index_groups=line)
    source = own_ids // count
    dy = (own_ids // per_owner - y_index + Y) % Y
    inside = own_ids % per_owner
    octet = jnp.array([0, 1, 2, 0])[dy]
    x_slot = jnp.array([0, 2, 3, 1])[(inside - 4 - dp_index + 2 * dp_count) % dp_count]
    place = jnp.where(
        dy == 0,
        inside,
        jnp.where(inside < 4, per_owner + octet * 4 + inside, per_owner + 12 + x_slot * 3 + octet),
    )
    left_near = ring_near(left_mixed, shift_dp)
    right_mixed = ring_mix(right_parts, right_far)
    right_near = ring_near(right_mixed, along_y)
    received, left_near, right_near = lax.optimization_barrier((received, left_near, right_near))
    left_x = ring_end(left_parts, left_near).astype(jnp.bfloat16)
    right_y = ring_end(right_parts, right_near).astype(jnp.bfloat16)
    query_cot = pl.pallas_call(
        tail_kernel,
        out_shape=jax.ShapeDtypeStruct((group_rows, 2 * half), jnp.bfloat16),
        in_specs=[SMEM, SMEM] + [VMEM] * 5,
        out_specs=VMEM,
        scratch_shapes=[pltpu.VMEM((picks, group_rows), jnp.float32)],
        compiler_params=pltpu.CompilerParams(vmem_limit_bytes=24 * 1024 * 1024),
        name="tail",
    )(source, place, received, probs, q_t, own_keys, second_table)

    cots = [query_cot] + [shift_dp(query_cot, d) for d in (1, 2, 3)]
    partial_grad = jnp.dot(
        inputs,
        jnp.concatenate(cots, axis=0),
        preferred_element_type=jnp.float32,
    )
    partial_grad = partial_grad.astype(jnp.bfloat16).reshape(mem_count, -1, 2 * half)
    spread = lax.all_to_all(partial_grad, "mem", 0, 0, tiled=True)
    query_grad = jnp.sum(spread.astype(jnp.float32), axis=0)

    left_y = ring_sum(left_x.reshape(Y, -1, cols), along_y)
    right_x = ring_sum(right_y.reshape(dp_count, -1, cols), shift_dp)
    value_grad = jnp.concatenate(
        [left_y.astype(jnp.bfloat16), right_x.astype(jnp.bfloat16)], axis=1
    )

    input_grad = lax.dot_general(query_cot, weight, NT, preferred_element_type=jnp.float32)
    handed = lax.ppermute(input_grad.astype(jnp.bfloat16), "section", [(0, 1), (1, 0)])
    return (value_grad[None], query_grad[None], handed[None])


def solution(mesh):
    placed = (
        P("section", ("mem", "dp"), None),
        P("section", ("mem", "dp"), None),
        P("section", None, None),
        P("section", None, None),
        P("section", None, None),
        P("section", "mem", None),
        P("section", None, None),
    )
    return jax.shard_map(
        shards,
        mesh=mesh,
        in_specs=placed,
        out_specs=(
            P("section", ("mem", "dp"), None),
            P("section", ("mem", "dp"), None),
            P("section", ("mem", "dp"), None),
        ),
        check_vma=False,
    )
```

```python
import functools
import math

import jax
import jax.numpy as jnp
from jax import lax
from jax.experimental import pallas as pl
from jax.experimental.pallas import tpu as pltpu
from jax.sharding import PartitionSpec as P

EPS = 1e-06
HIGHEST = lax.Precision.HIGHEST
VMEM = pl.BlockSpec(memory_space=pltpu.VMEM)
SMEM = pl.BlockSpec(memory_space=pltpu.SMEM)
NT = (((1,), (1,)), ((), ()))
Y = 4
TAIL = 16
LANES = 128


def shift_mem(block, dz, dy):
    count = lax.axis_size("mem")
    depth = count // Y
    route = []
    for z in range(depth):
        for y in range(Y):
            route.append((z * Y + y, ((z + dz) % depth) * Y + (y + dy) % Y))
    return lax.ppermute(block, "mem", route)


def shift_dp(block, step):
    count = lax.axis_size("dp")
    return lax.ppermute(block, "dp", [(i, (i + step) % count) for i in range(count)])


def normed(part):
    scale = lax.rsqrt(jnp.mean(part * part, axis=0, keepdims=True) + EPS)
    return part * scale, scale


def head_kernel(ids, x_ref, w_ref, k1_ref, k2_ref, up_ref, probs_ref, q_ref, keys_ref, load_ref):
    picks, half = keys_ref.shape
    q = jnp.dot(x_ref[...], w_ref[...], preferred_element_type=jnp.float32)
    q = q.astype(jnp.bfloat16).astype(jnp.float32)
    q_t = q.T
    q_ref[...] = q_t
    for k in range(picks):
        keys_ref[k : k + 1, :] = k1_ref[pl.ds(ids[k], 1), :]
    factor = 1.0 / math.sqrt(half)
    first, _ = normed(q_t[:half])
    second, _ = normed(q_t[half:])
    block_exp = jnp.exp(
        jnp.dot(keys_ref[...], first, precision=HIGHEST, preferred_element_type=jnp.float32) * factor
    )
    row_exp = jnp.exp(
        jnp.dot(k2_ref[...], second, precision=HIGHEST, preferred_element_type=jnp.float32) * factor
    )
    probs_ref[:picks, :] = block_exp / jnp.sum(block_exp, axis=0, keepdims=True)
    probs_ref[picks:, :] = row_exp / jnp.sum(row_exp, axis=0, keepdims=True)
    tokens = up_ref.shape[0]
    load_ref[:tokens, :] = up_ref[...]
    load_ref[tokens:, :] = jnp.zeros((TAIL, up_ref.shape[1]), jnp.bfloat16)
    tiles = probs_ref.shape[0] // TAIL
    for i in range(tiles):
        tile = probs_ref[i * TAIL : (i + 1) * TAIL, :]
        high = tile.astype(jnp.bfloat16)
        low = (tile - high.astype(jnp.float32)).astype(jnp.bfloat16)
        load_ref[tokens:, i * LANES : (i + 1) * LANES] = high
        load_ref[tokens:, (tiles + i) * LANES : (tiles + i + 1) * LANES] = low


def tail_kernel(source, place, recv_ref, probs_ref, q_ref, keys_ref, k2_ref, out_ref, cot_ref):
    picks, half = keys_ref.shape
    rows = k2_ref.shape[0]
    factor = 1.0 / math.sqrt(half)
    row_cot = jnp.sum(recv_ref[:, :rows, :], axis=0)
    for k in range(picks):
        cot_ref[k : k + 1, :] = recv_ref[source[k], pl.ds(rows + place[k], 1), :]
    block_cot = cot_ref[...]
    q_t = q_ref[...]

    def through(part, probs, cot, keys):
        unit, scale = normed(part)
        logit_cot = probs * (cot - jnp.sum(probs * cot, axis=0, keepdims=True)) * factor
        unit_cot = jnp.dot(
            keys.T, logit_cot, precision=HIGHEST, preferred_element_type=jnp.float32
        )
        inner = jnp.mean(unit * unit_cot, axis=0, keepdims=True)
        return scale * (unit_cot - unit * inner)

    lead = through(q_t[:half], probs_ref[:picks, :], block_cot, keys_ref[...])
    trail = through(q_t[half:], probs_ref[picks:, :], row_cot, k2_ref[...])
    out_ref[:, :half] = lead.T.astype(jnp.bfloat16)
    out_ref[:, half:] = trail.T.astype(jnp.bfloat16)


def table_kernel(chosen_ref, low_ref, rp_ref, *slot_refs):
    picks = chosen_ref.shape[2]
    tiles = (picks + rp_ref.shape[1]) // TAIL
    each = slot_refs[0].shape[1]
    for g in range(low_ref.shape[0]):

        def tile(i):
            high = low_ref[g, :, i * LANES : (i + 1) * LANES].astype(jnp.float32)
            rest = low_ref[g, :, (tiles + i) * LANES : (tiles + i + 1) * LANES]
            return high + rest.astype(jnp.float32)

        first = picks // TAIL
        block_probs = jnp.concatenate([tile(i) for i in range(first)], axis=0)
        for i in range(first, tiles):
            rp_ref[g, (i - first) * TAIL : (i - first + 1) * TAIL, :] = tile(i)
        slots = jnp.dot(
            chosen_ref[g], block_probs, precision=HIGHEST, preferred_element_type=jnp.float32
        )
        for n, ref in enumerate(slot_refs):
            ref[g] = slots[n * each : (n + 1) * each]


def return_kernel(up_ref, rp_ref, sp_ref, v_ref, out_ref, flat_ref):
    groups, rows, group_rows = rp_ref.shape
    blocks = sp_ref.shape[1]
    step = pl.program_id(0)

    @pl.when(step == 0)
    def _():
        for g in range(groups):
            flat_ref[g * group_rows : (g + 1) * group_rows, :] = up_ref[g, :group_rows, :]
            out_ref[g, :rows, :] = jnp.zeros((rows, group_rows), jnp.float32)

    products = lax.dot_general(v_ref[...], flat_ref[...], NT, preferred_element_type=jnp.float32)
    slots = pl.ds(pl.multiple_of(rows + step * blocks, blocks), blocks)
    for g in range(groups):
        row_probs = rp_ref[g]
        total = out_ref[g, :rows, :]
        sums = []
        for b in range(blocks):
            part = products[b * rows : (b + 1) * rows, g * group_rows : (g + 1) * group_rows]
            total = total + part * sp_ref[g, b : b + 1, :]
            sums.append(jnp.sum(part * row_probs, axis=0, keepdims=True))
        out_ref[g, :rows, :] = total
        out_ref[g, slots, :] = jnp.concatenate(sums, axis=0)


def cotangents(up, row_probs, slot_probs, held):
    groups, rows, group_rows = row_probs.shape
    slots = slot_probs.shape[1]
    width = up.shape[2]
    each = 8
    return pl.pallas_call(
        return_kernel,
        out_shape=jax.ShapeDtypeStruct((groups, rows + slots, group_rows), jnp.float32),
        grid=(slots // each,),
        in_specs=[
            pl.BlockSpec(up.shape, lambda i: (0, 0, 0)),
            pl.BlockSpec(row_probs.shape, lambda i: (0, 0, 0)),
            pl.BlockSpec((groups, each, group_rows), lambda i: (0, i, 0)),
            pl.BlockSpec((each * rows, width), lambda i: (i, 0)),
        ],
        out_specs=pl.BlockSpec((groups, rows + slots, group_rows), lambda i: (0, 0, 0)),
        scratch_shapes=[pltpu.VMEM((groups * group_rows, width), jnp.bfloat16)],
        compiler_params=pltpu.CompilerParams(vmem_limit_bytes=40 * 1024 * 1024),
        cost_estimate=pl.CostEstimate(
            flops=2 * groups * group_rows * slots * rows * width,
            bytes_accessed=2 * (groups * group_rows + slots * rows) * width,
            transcendentals=0,
        ),
        name="returns",
    )(up, row_probs, slot_probs, held)


def sum_kernel(rows, rp_ref, sp_ref, up_ref, out_ref, tile_ref, flat_ref):
    groups = rp_ref.shape[0]
    group_rows = rp_ref.shape[2]

    @pl.when(pl.program_id(0) == 0)
    def _():
        for g in range(groups):
            flat_ref[g * group_rows : (g + 1) * group_rows, :] = up_ref[g, :group_rows, :]

    for g in range(groups):
        row_probs = rp_ref[g]
        for b in range(sp_ref.shape[1]):
            tile_ref[b * rows : (b + 1) * rows, g * group_rows : (g + 1) * group_rows] = (
                sp_ref[g, b : b + 1, :] * row_probs
            ).astype(jnp.bfloat16)
    out_ref[...] = jnp.dot(
        tile_ref[...], flat_ref[...], preferred_element_type=jnp.float32
    ).astype(jnp.bfloat16)


def value_sums(row_probs, slot_probs, up, part):
    groups, rows, group_rows = row_probs.shape
    blocks = slot_probs.shape[1]
    tokens = groups * group_rows
    cols = up.shape[2] // 2
    each = 8
    return pl.pallas_call(
        functools.partial(sum_kernel, rows),
        out_shape=jax.ShapeDtypeStruct((blocks * rows, cols), jnp.bfloat16),
        grid=(blocks // each,),
        in_specs=[
            pl.BlockSpec((groups, rows, group_rows), lambda i: (0, 0, 0)),
            pl.BlockSpec((groups, each, group_rows), lambda i: (0, i, 0)),
            pl.BlockSpec((groups, up.shape[1], cols), lambda i: (0, 0, part)),
        ],
        out_specs=pl.BlockSpec((each * rows, cols), lambda i: (i, 0)),
        scratch_shapes=[
            pltpu.VMEM((each * rows, tokens), jnp.bfloat16),
            pltpu.VMEM((tokens, cols), jnp.bfloat16),
        ],
        compiler_params=pltpu.CompilerParams(vmem_limit_bytes=32 * 1024 * 1024),
        cost_estimate=pl.CostEstimate(
            flops=2 * blocks * rows * tokens * cols,
            bytes_accessed=2 * (tokens * cols + blocks * rows * cols),
            transcendentals=0,
        ),
        name="value_sums",
    )(row_probs, slot_probs, up)


def ring_gather(block, shift):
    low = shift(block, 1)
    high = shift(block, -1)
    cut = block.shape[0] // 2
    far = (shift(low[:cut], 1), shift(high[cut:], -1))
    return low, high, far


def wide(a):
    return a.astype(jnp.float32)


def ring_far(parts, shift):
    cut = parts.shape[1] // 2
    return shift(parts[2, :cut], 1), shift(parts[2, cut:], -1)


def ring_mix(parts, far):
    cut = parts.shape[1] // 2
    up = jnp.concatenate(
        [(wide(parts[1, :cut]) + wide(far[0])).astype(jnp.bfloat16), parts[1, cut:]], axis=0
    )
    down = jnp.concatenate(
        [parts[3, :cut], (wide(parts[3, cut:]) + wide(far[1])).astype(jnp.bfloat16)], axis=0
    )
    return up, down


def ring_near(mixed, shift):
    return shift(mixed[0], 1), shift(mixed[1], -1)


def ring_end(parts, near):
    return wide(parts[0]) + wide(near[0]) + wide(near[1])


def ring_sum(parts, shift):
    return ring_end(parts, ring_near(ring_mix(parts, ring_far(parts, shift)), shift))


def shards(layer_input, out_grad, query_weight, key_one, key_two, values, block_ids):
    tokens = layer_input[0]
    upstream = out_grad[0]
    weight = query_weight[0]
    first_table = key_one[0]
    second_table = key_two[0]
    all_ids = block_ids[0]
    group_rows, width = tokens.shape
    half = weight.shape[1] // 2
    rows = second_table.shape[0]
    per_owner = values.shape[1] // rows
    picks = all_ids.shape[1]
    mem_count = lax.axis_size("mem")
    dp_count = lax.axis_size("dp")
    depth = mem_count // Y
    mem_index = lax.axis_index("mem")
    dp_index = lax.axis_index("dp")
    z_index = mem_index // Y
    y_index = mem_index % Y
    own_ids = lax.dynamic_index_in_dim(all_ids, mem_index * dp_count + dp_index, 0, keepdims=False)
    cols = width // 2
    line = [[z * Y + y for z in range(depth)] for y in range(Y)]
    along_y = lambda block, step: shift_mem(block, 0, step)


    own_values = values[0]
    direct_rows = 4 * rows
    one_block = lax.dynamic_slice_in_dim(own_values, direct_rows + dp_index * rows, rows, 0)
    low_b, high_b, far_b = ring_gather(one_block, along_y)
    direct, far_b = lax.optimization_barrier((own_values[:direct_rows], far_b))
    low_d = along_y(direct, 1)
    high_d = along_y(direct, -1)
    spread_x = jnp.concatenate([low_b, high_b, *far_b], axis=0)

    probs, q_t, own_keys, load = pl.pallas_call(
        head_kernel,
        out_shape=(
            jax.ShapeDtypeStruct((picks + rows, group_rows), jnp.float32),
            jax.ShapeDtypeStruct((2 * half, group_rows), jnp.float32),
            jax.ShapeDtypeStruct((picks, half), jnp.float32),
            jax.ShapeDtypeStruct((group_rows + TAIL, width), jnp.bfloat16),
        ),
        in_specs=[SMEM] + [VMEM] * 5,
        out_specs=(VMEM,) * 4,
        compiler_params=pltpu.CompilerParams(vmem_limit_bytes=56 * 1024 * 1024),
        name="head",
    )(own_ids, tokens, weight, first_table, second_table, upstream)

    gathered = lax.all_gather(load, "mem", axis=0, axis_index_groups=line)

    cut = direct_rows // 2
    far_d = (along_y(low_d[:cut], 1), along_y(high_d[cut:], -1))
    low_x = shift_dp(spread_x, 1)
    high_x = shift_dp(spread_x, -1)
    late_tokens, low_x, high_x = lax.optimization_barrier((tokens, low_x, high_x))
    cut = spread_x.shape[0] // 2
    far_x = (shift_dp(low_x[:cut], 1), shift_dp(high_x[cut:], -1))

    y_at = (y_index + jnp.arange(Y)) % Y
    x_at = (dp_index + jnp.arange(dp_count)) % dp_count
    shard_base = (z_index * Y + y_at) * per_owner
    per_x = per_owner // dp_count
    x_blocks = x_at[:, None] * per_x + jnp.arange(per_x)[None, :]
    y_first = (shard_base[:, None, None] + x_blocks[None, :, :]).reshape(-1)
    x_first = (shard_base[None, :, None] + x_blocks[:, None, :]).reshape(-1)
    octets = shard_base[jnp.array([3, 1, 2])]
    x_held = x_at[jnp.array([0, 3, 1, 2])]
    held = jnp.concatenate(
        [
            shard_base[0] + jnp.arange(per_owner),
            (octets[:, None] + jnp.arange(4)[None, :]).reshape(-1),
            (octets[None, :] + 4 + x_held[:, None]).reshape(-1),
        ]
    )
    wanted = jnp.concatenate([held, x_first, y_first])
    cells = all_ids.reshape(depth, Y * dp_count, picks)
    line_ids = lax.dynamic_index_in_dim(cells, y_index * dp_count + dp_index, 1, keepdims=False)
    chosen = (line_ids[:, None, :] == wanted[None, :, None]).astype(jnp.float32)
    count = Y * per_owner
    slots = jax.ShapeDtypeStruct((depth, count, group_rows), jnp.float32)
    row_probs, held_probs, left_probs, right_probs = pl.pallas_call(
        table_kernel,
        out_shape=(jax.ShapeDtypeStruct((depth, rows, group_rows), jnp.float32),) + (slots,) * 3,
        grid=(1,),
        in_specs=[
            pl.BlockSpec(chosen.shape, lambda i: (0, 0, 0)),
            pl.BlockSpec((depth, TAIL, width), lambda i: (0, group_rows // TAIL, 0)),
        ],
        out_specs=(
            pl.BlockSpec((depth, rows, group_rows), lambda i: (0, 0, 0)),
        )
        + (pl.BlockSpec(slots.shape, lambda i: (0, 0, 0)),) * 3,
        name="tables",
    )(chosen, gathered)
    left_sums = value_sums(row_probs, left_probs, gathered, 0)
    right_sums = value_sums(row_probs, right_probs, gathered, 1)

    turned = late_tokens.T.reshape(mem_count, dp_count, width // (mem_count * dp_count), group_rows)
    turned = turned.transpose(1, 0, 2, 3).reshape(dp_count, width // dp_count, group_rows)

    def piece(offset):
        return lax.dynamic_index_in_dim(turned, (dp_index + offset) % dp_count, 0, keepdims=False)

    inputs = [piece(0)] + [shift_dp(piece(d), d) for d in (1, 2, 3)]
    inputs = jnp.concatenate(inputs, axis=1)
    left_parts = left_sums.reshape(dp_count, -1, cols)
    right_parts = right_sums.reshape(Y, -1, cols)
    left_far = ring_far(left_parts, shift_dp)
    right_far = ring_far(right_parts, along_y)
    left_mixed = ring_mix(left_parts, left_far)
    held_probs, inputs, left_mixed = lax.optimization_barrier((held_probs, inputs, left_mixed))
    left_sums, far_d, far_x = lax.optimization_barrier((left_sums, far_d, far_x))
    held_values = jnp.concatenate(
        [own_values, low_d, high_d, *far_d, spread_x, low_x, high_x, *far_x], axis=0
    )
    returned = cotangents(gathered, row_probs, held_probs, held_values)

    received = lax.all_to_all(returned, "mem", 0, 0, tiled=True, axis_index_groups=line)
    source = own_ids // count
    dy = (own_ids // per_owner - y_index + Y) % Y
    inside = own_ids % per_owner
    octet = jnp.array([0, 1, 2, 0])[dy]
    x_slot = jnp.array([0, 2, 3, 1])[(inside - 4 - dp_index + 2 * dp_count) % dp_count]
    place = jnp.where(
        dy == 0,
        inside,
        jnp.where(inside < 4, per_owner + octet * 4 + inside, per_owner + 12 + x_slot * 3 + octet),
    )
    left_x = ring_end(left_parts, ring_near(left_mixed, shift_dp)).astype(jnp.bfloat16)
    right_mixed = ring_mix(right_parts, right_far)
    right_near = ring_near(right_mixed, along_y)
    received, left_x, right_near = lax.optimization_barrier((received, left_x, right_near))
    right_y = ring_end(right_parts, right_near).astype(jnp.bfloat16)
    query_cot = pl.pallas_call(
        tail_kernel,
        out_shape=jax.ShapeDtypeStruct((group_rows, 2 * half), jnp.bfloat16),
        in_specs=[SMEM, SMEM] + [VMEM] * 5,
        out_specs=VMEM,
        scratch_shapes=[pltpu.VMEM((picks, group_rows), jnp.float32)],
        compiler_params=pltpu.CompilerParams(vmem_limit_bytes=24 * 1024 * 1024),
        name="tail",
    )(source, place, received, probs, q_t, own_keys, second_table)

    cots = [query_cot] + [shift_dp(query_cot, d) for d in (1, 2, 3)]
    partial_grad = jnp.dot(
        inputs,
        jnp.concatenate(cots, axis=0),
        preferred_element_type=jnp.float32,
    )
    partial_grad = partial_grad.astype(jnp.bfloat16).reshape(mem_count, -1, 2 * half)
    spread = lax.all_to_all(partial_grad, "mem", 0, 0, tiled=True)
    query_grad = jnp.sum(spread.astype(jnp.float32), axis=0)

    left_y = ring_sum(left_x.reshape(Y, -1, cols), along_y)
    right_x = ring_sum(right_y.reshape(dp_count, -1, cols), shift_dp)
    value_grad = jnp.concatenate(
        [left_y.astype(jnp.bfloat16), right_x.astype(jnp.bfloat16)], axis=1
    )

    input_grad = lax.dot_general(query_cot, weight, NT, preferred_element_type=jnp.float32)
    handed = lax.ppermute(input_grad.astype(jnp.bfloat16), "section", [(0, 1), (1, 0)])
    return (value_grad[None], query_grad[None], handed[None])


def solution(mesh):
    placed = (
        P("section", ("mem", "dp"), None),
        P("section", ("mem", "dp"), None),
        P("section", None, None),
        P("section", None, None),
        P("section", None, None),
        P("section", "mem", None),
        P("section", None, None),
    )
    return jax.shard_map(
        shards,
        mesh=mesh,
        in_specs=placed,
        out_specs=(
            P("section", ("mem", "dp"), None),
            P("section", ("mem", "dp"), None),
            P("section", ("mem", "dp"), None),
        ),
        check_vma=False,
    )
```
